256 devices in a mesh: seq: 16 (over y, x), tp: 16 (over z, core).
Axes of the slice: x: 4, y: 4, z: 8, core: 2. Of those that a mesh axis runs over, the one named last changes fastest.
Arguments:
- block_in: bfloat16 [2048, 8192], P(None, 'seq'), may hold values from -6 to 6
- w_in: bfloat16 [3, 8192, 8192], P(None, 'seq', 'tp'), may hold values from -0.0625 to 0.0625
- filt: float32 [512, 128], P('tp'), may hold values from -0.5 to 0.5
- skip: float32 [8192], P('tp'), may hold values from -3 to 3
- grad_y: bfloat16 [2048, 8192], P('seq', 'tp'), may hold values from -6 to 6
Outputs:
- block_out: bfloat16 [2048, 8192], P('seq', 'tp')
- grad_x: bfloat16 [2048, 8192], P('tp', 'seq')
- grad_w: float32 [3, 8192, 8192], P(None, 'seq', 'tp')
- grad_filt: float32 [512, 128], P('tp')
- grad_skip: float32 [8192], P('tp')
The draws below stay inside these ranges and needn't reach their ends.
All inputs are finite; a program needn't handle non-finite values.
Results may differ from the reference program's by a relative error of at most 0.025.
Values may be sent and summed in bfloat16 or wider, within the bound.
A program may use at most 128 MiB of HBM per device.

```python
import jax
import jax.numpy as jnp
from jax import lax

D = 8192
K = 128
GROUP_CH = 16
TOKENS = 2048
GROUPS = 512


def strengthened(result, stream_key, source, target, parts, factor):
    def block_of(axis_at):
        return (jnp.arange(result.shape[axis_at]) // (result.shape[axis_at] // parts)).reshape((-1,) + (1,) * (result.ndim - 1 - axis_at))

    first = jax.random.permutation(stream_key, parts)[block_of(target)]
    other_side = (block_of(target) + parts // 2) % parts
    return jnp.where((block_of(source) == first) | (block_of(source) == other_side), factor * result, result)


def block_scale(stream_key, shape, cuts, smallest, high):
    factor_of, own = 1.0, jax.random.fold_in(stream_key, 6)
    for dim, shards_of in cuts:
        steps = jnp.exp(jax.random.uniform(jax.random.fold_in(own, dim), (shards_of,), jnp.float32, smallest / len(cuts), high / len(cuts)))
        factor_of = factor_of * jnp.repeat(steps, shape[dim] // shards_of).reshape([-1 if axis == dim else 1 for axis in range(len(shape))])
    return factor_of


def noise(key, extent, deviation, reach, pieces=(), kind=jnp.bfloat16):
    result = deviation * jax.random.normal(key, extent, jnp.float32)
    if pieces:
        result = result * block_scale(key, extent, pieces, -0.22, 0.18)
    return jnp.clip(result, -reach, reach).astype(kind)


def heavy_noise(stream_key, shape, scale, most, pieces, heavy, kind=jnp.bfloat16):
    entries = scale * jax.random.normal(stream_key, shape, jnp.float32)
    if pieces:
        entries = entries * block_scale(stream_key, shape, pieces, -0.22, 0.18)
    return jnp.clip(strengthened(entries, jax.random.fold_in(stream_key, 3), *heavy), -most, most).astype(kind)


def setup_inputs(seed: int = 0) -> dict:
    seeds = jax.random.split(jax.random.key(seed), 6)
    return {
        "block_in": heavy_noise(seeds[0], (TOKENS, D), 1.0, 6.0, ((1, 16),), (1, 0, 16, 2.0)),
        "w_in": noise(seeds[1], (3, D, D), D ** -0.5, 0.0625, ((1, 16), (2, 16))),
        "filt": noise(seeds[2], (GROUPS, K), K ** -0.5, 0.5, ((0, 16),), jnp.float32),
        "skip": noise(seeds[3], (D,), 0.5, 3.0, ((0, 16),), jnp.float32),
        "grad_y": noise(seeds[4], (TOKENS, D), 1.0, 6.0, ((0, 16), (1, 16))),
    }


def reference(block_in, w_in, filt, skip, grad_y):
    proj = [jnp.dot(block_in, w_in[j], preferred_element_type=jnp.float32).astype(jnp.bfloat16) for j in range(3)]
    gate = proj[0].astype(jnp.float32)
    key = proj[1].astype(jnp.float32)
    value = proj[2].astype(jnp.float32)
    u = key * value
    taps = jnp.repeat(filt, GROUP_CH, axis=0).T
    padded_u = jnp.concatenate([jnp.zeros((K - 1, D), jnp.float32), u], axis=0)

    def causal_step(total, i):
        piece = lax.dynamic_slice_in_dim(padded_u, (K - 1 - i).astype(jnp.int32), TOKENS, 0)
        return (total + taps[i][None, :] * piece, None)
    conv, _ = lax.scan(causal_step, jnp.zeros((TOKENS, D), jnp.float32), jnp.arange(K, dtype=jnp.int32))
    z = conv + skip[None, :] * u
    block_out = (gate * z).astype(jnp.bfloat16)
    grad_out = grad_y.astype(jnp.float32)
    d_gate = grad_out * z
    dz = grad_out * gate
    padded_dz = jnp.concatenate([dz, jnp.zeros((K - 1, D), jnp.float32)], axis=0)

    def anti_step(total, i):
        piece = lax.dynamic_slice_in_dim(padded_dz, i.astype(jnp.int32), TOKENS, 0)
        return (total + taps[i][None, :] * piece, None)
    anti, _ = lax.scan(anti_step, jnp.zeros((TOKENS, D), jnp.float32), jnp.arange(K, dtype=jnp.int32))
    du = anti + skip[None, :] * dz

    def tap_grad(i):
        piece = lax.dynamic_slice_in_dim(padded_u, (K - 1 - i).astype(jnp.int32), TOKENS, 0)
        return lax.optimization_barrier(jnp.sum(dz * piece, axis=0))
    per_channel = lax.map(tap_grad, jnp.arange(K, dtype=jnp.int32))
    scale = TOKENS ** (-0.5)
    grad_filt = per_channel.reshape(K, GROUPS, GROUP_CH).sum(axis=2).T * scale
    grad_skip = lax.optimization_barrier(jnp.sum(dz * u, axis=0)) * scale
    dps = [d_gate.astype(jnp.bfloat16), (du * value).astype(jnp.bfloat16), (du * key).astype(jnp.bfloat16)]
    grad_in = jnp.zeros((TOKENS, D), jnp.float32)
    for j in range(3):
        grad_in = grad_in + jnp.dot(dps[j], w_in[j].T, preferred_element_type=jnp.float32)
    grad_x = grad_in.astype(jnp.bfloat16)
    grad_w = jnp.stack([jnp.dot(block_in.T, dps[j], preferred_element_type=jnp.float32) for j in range(3)], axis=0) * scale
    return (block_out, grad_x, grad_w, grad_filt, grad_skip)
```

```python
import functools

import jax
import jax.numpy as jnp
from jax import lax
from jax.experimental import pallas as pl
from jax.experimental.pallas import tpu as pltpu
from jax.sharding import PartitionSpec as P

MESH = pl.DeviceIdType.MESH
F32 = jnp.float32
BF16 = jnp.bfloat16
HIGHEST = lax.Precision.HIGHEST
N_SEMS = 256
QUARTER = 512


def dot_nt(a, b, precision=None):
    return lax.dot_general(a, b, (((1,), (1,)), ((), ())), precision=precision, preferred_element_type=F32)


def dot_nn(a, b, precision=None):
    return lax.dot_general(a, b, (((1,), (0,)), ((), ())), precision=precision, preferred_element_type=F32)


def block_kernel(
    scale, bi, w, filt, skip, gy, bo_out, gx_out, gw_out, gf_out, gs_out,
    wt, bit, part, r1, r2, gath, gx, gyt, gy1, gy2, bo0, bo1, bo2, sm, cs, cr, zs, zr, ssem, rsem,
):
    seq, tp = lax.axis_index("seq"), lax.axis_index("tp")
    x, y, z, core = lax.rem(seq, 4), lax.div(seq, 4), lax.div(tp, 2), lax.rem(tp, 2)

    def m4(v):
        return lax.rem(v + 4, 4)

    def m8(v):
        return lax.rem(v + 8, 8)

    def at_x(by):
        return (y * 4 + m4(x + by), tp)

    def at_y(by):
        return (m4(y + by) * 4 + x, tp)

    def at_z(by):
        return (seq, m8(z + by) * 2 + core)

    at_core = (seq, z * 2 + (1 - core))
    partners = [at_x(1), at_x(-1), at_x(2), at_y(1), at_y(-1), at_y(2), at_z(1), at_z(-1), at_core]

    barrier = pltpu.get_barrier_semaphore()
    for device in partners:
        pl.semaphore_signal(barrier, inc=1, device_id=device, device_id_type=MESH)

    sent = []

    def send(src, dst, device):
        k = len(sent)
        copy = pltpu.make_async_remote_copy(
            src_ref=src, dst_ref=dst, send_sem=ssem.at[k], recv_sem=rsem.at[k], device_id=device, device_id_type=MESH
        )
        copy.start()
        sent.append(copy)
        return copy

    def transpose_w(g):
        for j in range(3):
            wt[j, g * 256 : (g + 1) * 256, :] = w[j, :, g * 256 : (g + 1) * 256].T

    def transpose_bi():
        @pl.loop(0, 4)
        def _(i):
            rows = pl.ds(pl.multiple_of(i * 512, 512), 512)
            bit[:, rows] = bi[rows, :].T

    def project(g):
        @pl.loop(0, 4)
        def _(i):
            rows = pl.ds(pl.multiple_of(i * 512, 512), 512)
            tokens = bi[rows, :]
            for j in range(3):
                p = dot_nt(wt[j, g * 256 : (g + 1) * 256, :], tokens).astype(BF16)
                part[g, j, :, :, :, rows] = p.reshape(4, 4, 16, 512)

    def grad_x_quarter(g, i):
        rows = pl.ds(i * QUARTER, QUARTER)
        total = None
        for j in range(3):
            d = gath[g, j, :, :, :, rows].reshape(256, QUARTER)
            p = dot_nn(w[j, :, g * 256 : (g + 1) * 256], d)
            total = p if total is None else total + p
        if g == 0:
            gx[:, rows] = total
        else:
            gx[:, rows] += total

    def grad_w(g, j):
        for i in range(2):
            d = gath[g, j].reshape(256, 2048)
            gw_out[j, i * 256 : (i + 1) * 256, g * 256 : (g + 1) * 256] = dot_nt(bit[i * 256 : (i + 1) * 256, :], d) * scale

    pos_big, pos_small = (x, y), (y, x)
    big_dev, small_dev = (at_x, at_y), (at_y, at_x)

    def big(ref, g, h, q, start, size):
        tokens = pl.ds(h * 1024 + start, size)
        return ref.at[g, :, :, q, :, tokens] if h == 0 else ref.at[g, :, q, :, :, tokens]

    def one(ref, g, h, q_big, q_small, start, size):
        tokens = pl.ds(h * 1024 + start, size)
        return ref.at[g, :, q_small, q_big, :, tokens] if h == 0 else ref.at[g, :, q_big, q_small, :, tokens]

    def small(g, h, q, start, size):
        return one(part, g, h, pos_big[h], q, start, size)

    BY = (1, -1)
    FAR = (0, QUARTER)
    NEAR = (QUARTER, 0)

    def add_big(dst, *srcs):
        @pl.loop(0, 3)
        def _(j):
            for i in range(4):
                total = dst[j, i].astype(F32)
                for s in srcs:
                    total = total + s[j, i].astype(F32)
                dst[j, i] = total.astype(BF16)

    def add_small(dst, *srcs):
        for j in range(3):
            total = dst[j].astype(F32)
            for s in srcs:
                total = total + s[j].astype(F32)
            dst[j] = total.astype(BF16)

    s1, s2a, s2b, t1, t2a, t2b = {}, {}, {}, {}, {}, {}

    def send_s1(g):
        for h in range(2):
            for d in range(2):
                src = big(part, g, h, m4(pos_big[h] + 2), FAR[d], QUARTER)
                s1[g, h, d] = send(src, r1.at[g, h, d, 0], big_dev[h](BY[d]))

    def send_s2a(g):
        for h in range(2):
            for d in range(2):
                src = big(part, g, h, m4(pos_big[h] + BY[d]), NEAR[d], QUARTER)
                s2a[g, h, d] = send(src, r1.at[g, h, d, 1], big_dev[h](BY[d]))

    def send_s2b(g):
        for h in range(2):
            for d in range(2):
                src = big(part, g, h, m4(pos_big[h] + BY[d]), FAR[d], QUARTER)
                s1[g, h, d].wait_recv()
                add_big(src, r1.at[g, h, d, 0])
                s2b[g, h, d] = send(src, r1.at[g, h, d, 2], big_dev[h](BY[d]))

    def finish_big(g):
        for h in range(2):
            for d in range(2):
                s2a[g, h, d].wait_recv()
        for h in range(2):
            for d in range(2):
                s2b[g, h, d].wait_recv()
                add_big(big(part, g, h, pos_big[h], FAR[d], QUARTER), r1.at[g, h, d, 2], r1.at[g, h, 1 - d, 1])
                t1[g, h, d] = send(small(g, h, m4(pos_small[h] + 2), FAR[d], QUARTER), r2.at[g, h, d, 0], small_dev[h](BY[d]))
                src = small(g, h, m4(pos_small[h] + BY[1 - d]), FAR[d], QUARTER)
                t2a[g, h, 1 - d] = send(src, r2.at[g, h, 1 - d, 1], small_dev[h](BY[1 - d]))

    def send_t2b(g):
        for h in range(2):
            for d in range(2):
                t1[g, h, d].wait_recv()
                src = small(g, h, m4(pos_small[h] + BY[d]), FAR[d], QUARTER)
                add_small(src, r2.at[g, h, d, 0])
                t2b[g, h, d] = send(src, r2.at[g, h, d, 2], small_dev[h](BY[d]))

    def filter_group(g):
        for h in range(2):
            for d in range(2):
                t2a[g, h, d].wait_recv()
                t2b[g, h, d].wait_recv()

        def stacked(j):
            pieces = []
            for b in range(16):
                h, d, o = b // 8, (b % 8) // 4, (b % 4) * 128
                total = part[g, j, y, x, :, b * 128 : (b + 1) * 128].astype(F32)
                total = total + r2[g, h, d, 2, j, :, o : o + 128].astype(F32)
                total = total + r2[g, h, 1 - d, 1, j, :, o : o + 128].astype(F32)
                pieces.append(total.astype(BF16).astype(F32))
            return jnp.concatenate(pieces, axis=0)

        gate, key, value = stacked(0), stacked(1), stacked(2)
        u = key * value
        blank = jnp.zeros((16, 128), F32)
        u_ext = jnp.concatenate([jnp.concatenate([blank, u[:240]], axis=0), u], axis=1)
        taps = jnp.broadcast_to(filt[pl.ds(g * 16 + seq, 1), :], (256, 128))
        taps = jnp.concatenate([taps, jnp.zeros((256, 128), F32)], axis=1)
        causal = pltpu.roll(taps, 128, 1, stride=1, stride_axis=0)[:, :128]
        anti = pltpu.roll(taps[:128], 0, 1, stride=1, stride_axis=0)

        lane = lax.broadcasted_iota(jnp.int32, (16, 512), 1)
        row = lax.broadcasted_iota(jnp.int32, (16, 512), 0)
        mine = lane == row + (g * 256 + seq * 16)
        skip_col = jnp.sum(jnp.where(mine, jnp.broadcast_to(skip[...], (16, 512)), 0.0), axis=1, keepdims=True)
        skip_all = jnp.concatenate([jnp.broadcast_to(skip_col, (16, 128))] * 16, axis=0)

        z_val = dot_nn(u_ext, causal, HIGHEST) + skip_all * u
        g_y = jnp.concatenate([gy2[b // 4, b % 4, g] for b in range(16)], axis=0).astype(F32)
        dz = g_y * gate
        dz_ext = jnp.concatenate([dz, jnp.concatenate([dz[16:], blank], axis=0)], axis=1)
        du = dot_nt(dz_ext, anti, HIGHEST) + skip_all * dz

        def keep(j, value_of):
            v = value_of.astype(BF16)
            for b in range(16):
                gath[g, j, y, x, :, b * 128 : (b + 1) * 128] = v[b * 16 : (b + 1) * 16]

        keep(0, g_y * z_val)
        keep(1, du * value)
        keep(2, du * key)
        out = (gate * z_val).astype(BF16)
        for b in range(16):
            bo0[g, b // 4, b % 4] = out[b * 16 : (b + 1) * 16]

        def sums():
            flip = (lax.broadcasted_iota(jnp.int32, (128, 128), 0) + lax.broadcasted_iota(jnp.int32, (128, 128), 1)) == 127
            dz_back = dot_nt(jnp.where(flip, 1.0, 0.0).astype(F32), dz, HIGHEST)
            lagged = pltpu.roll(dot_nn(dz_back, u_ext, HIGHEST), 129, 1, stride=1, stride_axis=0)
            by_lag = jnp.broadcast_to(jnp.sum(lagged, axis=0, keepdims=True), (8, 256))
            lag_rows = lax.broadcasted_iota(jnp.int32, (256, 128), 0)
            lag_cols = lax.broadcasted_iota(jnp.int32, (256, 128), 1)
            pick = jnp.where(lag_rows + lag_cols == 128, 1.0, 0.0).astype(F32)
            sm[y, x, g : g + 1, :] = dot_nn(by_lag, pick, HIGHEST)[:1] * scale
            product = dz * u
            folded = product[:16]
            for b in range(1, 16):
                folded = folded + product[b * 16 : (b + 1) * 16]
            per_ch = jnp.sum(folded, axis=1, keepdims=True) * scale
            placed = jnp.sum(jnp.where(mine, jnp.broadcast_to(per_ch, (16, 512)), 0.0), axis=0, keepdims=True)
            for i in range(2):
                o = g * 256 + i * 128
                sm[y, x, 4 + g * 2 + i : 5 + g * 2 + i, :] = placed[:, o : o + 128]

        return sums

    u1, u2, v1, v2 = {}, {}, {}, {}

    def ag_send(table, key, g, h, q_big, q_small, start, size, device):
        ref = one(gath, g, h, q_big, q_small, start, size)
        table[key] = send(ref, ref, device)

    def ag_open(g):
        for h in range(2):
            for d in range(2):
                ag_send(u1, (g, h, d), g, h, pos_big[h], pos_small[h], 0, 1024, small_dev[h](BY[d]))
        for h in range(2):
            for d in range(2):
                ag_send(v1, (g, h, 0, d), g, h, pos_big[h], pos_small[h], 0, 1024, big_dev[h](BY[d]))

    def ag_near(g):
        for h in range(2):
            for d in range(2):
                u1[g, h, d].wait_recv()
                ag_send(u2, (g, h, d), g, h, pos_big[h], m4(pos_small[h] - BY[d]), FAR[d], QUARTER, small_dev[h](BY[d]))
        for h in range(2):
            for e in range(2):
                for d in range(2):
                    ag_send(v1, (g, h, 1 + e, d), g, h, pos_big[h], m4(pos_small[h] - BY[e]), 0, 1024, big_dev[h](BY[d]))

    def ag_far(g):
        for h in range(2):
            for d in range(2):
                u2[g, h, d].wait_recv()
            for d in range(2):
                ag_send(v1, (g, h, 3, d), g, h, pos_big[h], m4(pos_small[h] + 2), 0, 1024, big_dev[h](BY[d]))

    def ag_forward(g, piece):
        for h in range(2):
            q = m4(pos_small[h] + (0, -1, 1, 2)[piece])
            for d in range(2):
                v1[g, h, piece, d].wait_recv()
                ag_send(v2, (g, h, piece, d), g, h, m4(pos_big[h] - BY[d]), q, FAR[d], QUARTER, big_dev[h](BY[d]))

    def ag_close(g):
        for h in range(2):
            for piece in range(4):
                for d in range(2):
                    v2[g, h, piece, d].wait_recv()

    def bo_first(g):
        own = bo0[g, y]
        bo1[g, y] = own
        return [send(bo0.at[g, m4(y + k)], bo1.at[g, y], at_y(k)) for k in (1, -1, 2)]

    def bo_second(g, arriving):
        for copy in arriving:
            copy.wait_recv()
        bo2[g, x] = bo1[g, :, x]
        return [send(bo1.at[g, :, m4(x + k)], bo2.at[g, x], at_x(k)) for k in (1, -1, 2)]

    def bo_last(g, arriving):
        for copy in arriving:
            copy.wait_recv()
        rows = jnp.concatenate([bo2[g, d % 4, d // 4] for d in range(16)], axis=0)
        bo_out[:, g * 256 : (g + 1) * 256] = rows.T

    gy_t = gy[...].T
    for g in range(2):
        for d in range(16):
            gyt[d % 4, d // 4, g] = gy_t[g * 256 + d * 16 : g * 256 + (d + 1) * 16]
    gy1[x] = gyt[x]
    transpose_w(0)
    project(0)
    pl.semaphore_wait(barrier, len(partners))
    gy_a = [send(gyt.at[m4(x + k)], gy1.at[x], at_x(k)) for k in (1, -1, 2)]
    send_s1(0)
    send_s2a(0)
    transpose_w(1)
    project(1)
    for copy in gy_a:
        copy.wait_recv()
    gy2[y] = gy1[:, y]
    gy_b = [send(gy1.at[:, m4(y + k)], gy2.at[y], at_y(k)) for k in (1, -1, 2)]
    send_s2b(0)
    transpose_bi()
    send_s1(1)
    sm[y, x] = jnp.zeros((8, 128), F32)
    finish_big(0)
    send_s2a(1)
    send_t2b(0)
    send_s2b(1)
    for copy in gy_b:
        copy.wait_recv()
    sums0 = filter_group(0)
    ag_open(0)
    sums0()
    finish_big(1)
    ag_near(0)
    bo_a0 = bo_first(0)
    send_t2b(1)
    ag_forward(0, 0)
    ag_far(0)
    bo_b0 = bo_second(0, bo_a0)
    sums1 = filter_group(1)
    ag_open(1)
    sums1()
    ag_forward(0, 1)
    ag_forward(0, 2)
    ag_near(1)
    ag_forward(0, 3)
    ag_far(1)
    bo_a1 = bo_first(1)
    sm_a = [send(sm.at[y, x], sm.at[y, x], at_y(k)) for k in (1, -1, 2)]
    ag_close(0)
    ag_forward(1, 0)
    grad_x_quarter(0, 0)
    grad_x_quarter(0, 1)
    ag_forward(1, 1)
    ag_forward(1, 2)
    grad_x_quarter(0, 2)
    grad_x_quarter(0, 3)
    bo_b1 = bo_second(1, bo_a1)
    for copy in sm_a:
        copy.wait_recv()
    sm_b = [send(sm.at[:, x], sm.at[:, x], at_x(k)) for k in (1, -1, 2)]
    ag_forward(1, 3)
    for j in range(3):
        grad_w(0, j)
    ag_close(1)

    order = (4, 3, -3, 2, -2, 1, -1, 0)
    pair = {}
    gx_other = [None] * 8
    for i in range(4):
        grad_x_quarter(1, i)
    for k in order:
        q = m8(z + k)
        theirs = pl.ds(pl.multiple_of((q * 2 + (1 - core)) * 128, 128), 128)
        cs[q] = gx[:, theirs].astype(BF16)
        pair[k] = send(cs.at[q], cr.at[q], at_core)

    def pair_sum(k):
        q = m8(z + k)
        own = pl.ds(pl.multiple_of((q * 2 + core) * 128, 128), 128)
        pair[k].wait_recv()
        zs[q] = (gx[:, own] + cr[q].astype(F32)).astype(BF16)

    ring = {}
    FARZ, NEARZ = (0, 256), (256, 0)

    def z_send(d, k, far, received):
        q = m8(z + BY[d] * k)
        r = (FARZ if far else NEARZ)[d]
        slot = (4 - k) if far else (4 + 3 - k)
        if received:
            prev = ring[d, k + 1, far]
            prev.wait_recv()
            rows = zs.at[q, r : r + 256]
            zs[q, r : r + 256] = (rows[...].astype(F32) + zr[d, slot - 1].astype(F32)).astype(BF16)
        ring[d, k, far] = send(zs.at[q, pl.ds(r, 256)], zr.at[d, slot], at_z(BY[d]))

    pair_sum(4)
    for d in range(2):
        z_send(d, 4, True, False)
    pair_sum(3)
    pair_sum(-3)
    for d in range(2):
        z_send(d, 3, False, False)
    for k in order[3:]:
        pair_sum(k)
    for d in range(2):
        z_send(d, 3, True, True)
    grad_w(1, 0)
    for k in (2, 1):
        for far in (False, True):
            for d in range(2):
                z_send(d, k, far, True)
        grad_w(1, 3 - k)
    bo_last(0, bo_b0)
    bo_last(1, bo_b1)
    for copy in sm_b:
        copy.wait_recv()
    for g in range(2):
        for d in range(16):
            gf_out[g * 16 + d : g * 16 + d + 1, :] = sm[d // 4, d % 4, g : g + 1, :]
    skips = sm[0, 0, 4:8, :]
    for d in range(1, 16):
        skips = skips + sm[d // 4, d % 4, 4:8, :]
    gs_out[...] = skips

    for far, rows in ((False, 0), (True, 0)):
        for d in range(2):
            ring[d, 1, far].wait_recv()
    own = zs[z]
    top = own[:256].astype(F32) + zr[0, 3].astype(F32) + zr[1, 6].astype(F32)
    low = own[256:].astype(F32) + zr[1, 3].astype(F32) + zr[0, 6].astype(F32)
    gx_out[:, :256] = top.T.astype(BF16)
    gx_out[:, 256:] = low.T.astype(BF16)
    for copy in sent:
        copy.wait_send()


def per_device(block_in, w_in, filt, skip, grad_y):
    tokens = block_in.shape[0]
    scale = tokens ** (-0.5)
    vmem = pl.BlockSpec(memory_space=pltpu.VMEM)
    out_shape = (
        jax.ShapeDtypeStruct((128, 512), BF16),
        jax.ShapeDtypeStruct((128, 512), BF16),
        jax.ShapeDtypeStruct((3, 512, 512), F32),
        jax.ShapeDtypeStruct((32, 128), F32),
        jax.ShapeDtypeStruct((4, 128), F32),
    )
    scratch = [
        pltpu.VMEM((3, 512, 512), BF16),
        pltpu.VMEM((512, 2048), BF16),
        pltpu.VMEM((2, 3, 4, 4, 16, 2048), BF16),
        pltpu.VMEM((2, 2, 2, 3, 3, 4, 16, QUARTER), BF16),
        pltpu.VMEM((2, 2, 2, 3, 3, 16, QUARTER), BF16),
        pltpu.VMEM((2, 3, 4, 4, 16, 2048), BF16),
        pltpu.VMEM((512, 2048), F32),
        pltpu.VMEM((4, 4, 2, 16, 128), BF16),
        pltpu.VMEM((4, 4, 2, 16, 128), BF16),
        pltpu.VMEM((4, 4, 2, 16, 128), BF16),
        pltpu.VMEM((2, 4, 4, 16, 128), BF16),
        pltpu.VMEM((2, 4, 4, 16, 128), BF16),
        pltpu.VMEM((2, 4, 4, 16, 128), BF16),
        pltpu.VMEM((4, 4, 8, 128), F32),
        pltpu.VMEM((8, 512, 128), BF16),
        pltpu.VMEM((8, 512, 128), BF16),
        pltpu.VMEM((8, 512, 128), BF16),
        pltpu.VMEM((2, 7, 256, 128), BF16),
        pltpu.SemaphoreType.DMA((N_SEMS,)),
        pltpu.SemaphoreType.DMA((N_SEMS,)),
    ]
    block_out, grad_x, grad_w, grad_filt, grad_skip = pl.pallas_call(
        functools.partial(block_kernel, scale),
        out_shape=out_shape,
        in_specs=[vmem] * 5,
        out_specs=[vmem] * 5,
        scratch_shapes=scratch,
        compiler_params=pltpu.CompilerParams(
            collective_id=0, has_side_effects=True, vmem_limit_bytes=60 * 2**20
        ),
        cost_estimate=pl.CostEstimate(flops=10**10, bytes_accessed=10**7, transcendentals=0),
    )(block_in, w_in, filt, skip.reshape(1, 512), grad_y)
    return block_out, grad_x, grad_w, grad_filt, grad_skip.reshape(512)


def solution(mesh):
    in_specs = (P(None, "seq"), P(None, "seq", "tp"), P("tp", None), P("tp"), P("seq", "tp"))
    out_specs = (P("seq", "tp"), P("tp", "seq"), P(None, "seq", "tp"), P("tp", None), P("tp"))
    return jax.shard_map(per_device, mesh=mesh, in_specs=in_specs, out_specs=out_specs, check_vma=False)
```

```python
import functools

import jax
import jax.numpy as jnp
from jax import lax
from jax.experimental import pallas as pl
from jax.experimental.pallas import tpu as pltpu
from jax.sharding import PartitionSpec as P

MESH = pl.DeviceIdType.MESH
F32 = jnp.float32
BF16 = jnp.bfloat16
HIGHEST = lax.Precision.HIGHEST
N_SEMS = 256
QUARTER = 512


def dot_nt(a, b, precision=None):
    return lax.dot_general(a, b, (((1,), (1,)), ((), ())), precision=precision, preferred_element_type=F32)


def dot_nn(a, b, precision=None):
    return lax.dot_general(a, b, (((1,), (0,)), ((), ())), precision=precision, preferred_element_type=F32)


def block_kernel(
    scale, bi_in, w_in, filt, skip, gy, bo_out, gx_out, gw_out, gf_out, gs_out,
    bi, w, wt, bit, part, r1, r2, gath, gx, gyt, gy1, gy2, bo0, bo1, bo2, sm, cs, cr, zs, zr, ssem, rsem, lsem,
):
    seq, tp = lax.axis_index("seq"), lax.axis_index("tp")
    x, y, z, core = lax.rem(seq, 4), lax.div(seq, 4), lax.div(tp, 2), lax.rem(tp, 2)

    def m4(v):
        return lax.rem(v + 4, 4)

    def m8(v):
        return lax.rem(v + 8, 8)

    def at_x(by):
        return (y * 4 + m4(x + by), tp)

    def at_y(by):
        return (m4(y + by) * 4 + x, tp)

    def at_z(by):
        return (seq, m8(z + by) * 2 + core)

    at_core = (seq, z * 2 + (1 - core))
    partners = [at_x(1), at_x(-1), at_x(2), at_y(1), at_y(-1), at_y(2), at_z(1), at_z(-1), at_core]

    barrier = pltpu.get_barrier_semaphore()
    for device in partners:
        pl.semaphore_signal(barrier, inc=1, device_id=device, device_id_type=MESH)

    def load(src, dst, k):
        copy = pltpu.make_async_copy(src, dst, lsem.at[k])
        copy.start()
        return copy

    half_w = [pl.ds(0, 256), pl.ds(256, 256)]
    quarter = [pl.ds(i * QUARTER, QUARTER) for i in range(4)]
    w_load = [load(w_in.at[:, :, half_w[0]], w.at[:, :, half_w[0]], 0)]
    bi_load = [load(bi_in.at[q], bi.at[q], 2 + i) for i, q in enumerate(quarter)]
    w_load.append(load(w_in.at[:, :, half_w[1]], w.at[:, :, half_w[1]], 1))

    sent = []

    def send(src, dst, device):
        k = len(sent)
        copy = pltpu.make_async_remote_copy(
            src_ref=src, dst_ref=dst, send_sem=ssem.at[k], recv_sem=rsem.at[k], device_id=device, device_id_type=MESH
        )
        copy.start()
        sent.append(copy)
        return copy

    def transpose_w(g):
        for j in range(3):
            wt[j, g * 256 : (g + 1) * 256, :] = w[j, :, g * 256 : (g + 1) * 256].T

    def transpose_bi():
        @pl.loop(0, 4)
        def _(i):
            rows = pl.ds(pl.multiple_of(i * 512, 512), 512)
            bit[:, rows] = bi[rows, :].T

    def project_rows(g, rows):
        tokens = bi[rows, :]
        for j in range(3):
            p = dot_nt(wt[j, g * 256 : (g + 1) * 256, :], tokens).astype(BF16)
            part[g, j, :, :, :, rows] = p.reshape(4, 4, 16, 512)

    def project(g):
        @pl.loop(0, 4)
        def _(i):
            project_rows(g, pl.ds(pl.multiple_of(i * 512, 512), 512))

    def grad_x_near(i):
        rows = quarter[i]
        total = None
        for j in range(3):
            p = dot_nn(w[j, :, :256], gath[0, j, :, :, :, rows].reshape(256, QUARTER))
            total = p if total is None else total + p
        gx[:, rows] = total

    def grad_x_chunk(q):
        rows = pl.ds(pl.multiple_of(q * 256, 256), 256)
        total = gx[:, rows]
        for j in range(3):
            total = total + dot_nn(w[j, :, 256:], gath[1, j, :, :, :, rows].reshape(256, 256))
        gx[:, rows] = total

    def grad_w(g, j, i):
        d = gath[g, j].reshape(256, 2048)
        gw_out[j, i * 256 : (i + 1) * 256, half_w[g]] = dot_nt(bit[i * 256 : (i + 1) * 256, :], d) * scale

    pos_big, pos_small = (x, y), (y, x)
    big_dev, small_dev = (at_x, at_y), (at_y, at_x)

    def big(ref, g, h, q, start, size):
        tokens = pl.ds(h * 1024 + start, size)
        return ref.at[g, :, :, q, :, tokens] if h == 0 else ref.at[g, :, q, :, :, tokens]

    def one(ref, g, h, q_big, q_small, start, size):
        tokens = pl.ds(h * 1024 + start, size)
        return ref.at[g, :, q_small, q_big, :, tokens] if h == 0 else ref.at[g, :, q_big, q_small, :, tokens]

    def small(g, h, q, start, size):
        return one(part, g, h, pos_big[h], q, start, size)

    BY = (1, -1)
    FAR = (0, QUARTER)
    NEAR = (QUARTER, 0)

    def add_big(dst, *srcs):
        @pl.loop(0, 3)
        def _(j):
            for i in range(4):
                total = dst[j, i].astype(F32)
                for s in srcs:
                    total = total + s[j, i].astype(F32)
                dst[j, i] = total.astype(BF16)

    def add_small(dst, *srcs):
        for j in range(3):
            total = dst[j].astype(F32)
            for s in srcs:
                total = total + s[j].astype(F32)
            dst[j] = total.astype(BF16)

    s1, s2a, s2b, t1, t2a, t2b = {}, {}, {}, {}, {}, {}

    def send_s1_one(g, h, d):
        src = big(part, g, h, m4(pos_big[h] + 2), FAR[d], QUARTER)
        s1[g, h, d] = send(src, r1.at[g, h, d, 0], big_dev[h](BY[d]))

    def send_s1(g):
        for h in range(2):
            for d in range(2):
                send_s1_one(g, h, d)

    def send_s2a(g):
        for h in range(2):
            for d in range(2):
                src = big(part, g, h, m4(pos_big[h] + BY[d]), NEAR[d], QUARTER)
                s2a[g, h, d] = send(src, r1.at[g, h, d, 1], big_dev[h](BY[d]))

    def send_s2b(g):
        for h in range(2):
            for d in range(2):
                src = big(part, g, h, m4(pos_big[h] + BY[d]), FAR[d], QUARTER)
                s1[g, h, d].wait_recv()
                add_big(src, r1.at[g, h, d, 0])
                s2b[g, h, d] = send(src, r1.at[g, h, d, 2], big_dev[h](BY[d]))

    def finish_big(g):
        for h in range(2):
            for d in range(2):
                s2a[g, h, d].wait_recv()
        for h in range(2):
            for d in range(2):
                s2b[g, h, d].wait_recv()
                add_big(big(part, g, h, pos_big[h], FAR[d], QUARTER), r1.at[g, h, d, 2], r1.at[g, h, 1 - d, 1])
                t1[g, h, d] = send(small(g, h, m4(pos_small[h] + 2), FAR[d], QUARTER), r2.at[g, h, d, 0], small_dev[h](BY[d]))
                src = small(g, h, m4(pos_small[h] + BY[1 - d]), FAR[d], QUARTER)
                t2a[g, h, 1 - d] = send(src, r2.at[g, h, 1 - d, 1], small_dev[h](BY[1 - d]))

    def send_t2b(g):
        for h in range(2):
            for d in range(2):
                t1[g, h, d].wait_recv()
                src = small(g, h, m4(pos_small[h] + BY[d]), FAR[d], QUARTER)
                add_small(src, r2.at[g, h, d, 0])
                t2b[g, h, d] = send(src, r2.at[g, h, d, 2], small_dev[h](BY[d]))

    def filter_group(g):
        for h in range(2):
            for d in range(2):
                t2a[g, h, d].wait_recv()
                t2b[g, h, d].wait_recv()

        def stacked(j):
            pieces = []
            for b in range(16):
                h, d, o = b // 8, (b % 8) // 4, (b % 4) * 128
                total = part[g, j, y, x, :, b * 128 : (b + 1) * 128].astype(F32)
                total = total + r2[g, h, d, 2, j, :, o : o + 128].astype(F32)
                total = total + r2[g, h, 1 - d, 1, j, :, o : o + 128].astype(F32)
                pieces.append(total.astype(BF16).astype(F32))
            return jnp.concatenate(pieces, axis=0)

        gate, key, value = stacked(0), stacked(1), stacked(2)
        u = key * value
        blank = jnp.zeros((16, 128), F32)
        u_ext = jnp.concatenate([jnp.concatenate([blank, u[:240]], axis=0), u], axis=1)
        taps = jnp.broadcast_to(filt[pl.ds(g * 16 + seq, 1), :], (256, 128))
        taps = jnp.concatenate([taps, jnp.zeros((256, 128), F32)], axis=1)
        causal = pltpu.roll(taps, 128, 1, stride=1, stride_axis=0)[:, :128]
        anti = pltpu.roll(taps[:128], 0, 1, stride=1, stride_axis=0)

        lane = lax.broadcasted_iota(jnp.int32, (16, 512), 1)
        row = lax.broadcasted_iota(jnp.int32, (16, 512), 0)
        mine = lane == row + (g * 256 + seq * 16)
        skip_col = jnp.sum(jnp.where(mine, jnp.broadcast_to(skip[...], (16, 512)), 0.0), axis=1, keepdims=True)
        skip_all = jnp.concatenate([jnp.broadcast_to(skip_col, (16, 128))] * 16, axis=0)

        z_val = dot_nn(u_ext, causal, HIGHEST) + skip_all * u
        g_y = jnp.concatenate([gy2[b // 4, b % 4, g] for b in range(16)], axis=0).astype(F32)
        dz = g_y * gate
        dz_ext = jnp.concatenate([dz, jnp.concatenate([dz[16:], blank], axis=0)], axis=1)
        du = dot_nt(dz_ext, anti, HIGHEST) + skip_all * dz

        def keep(j, value_of):
            v = value_of.astype(BF16)
            for b in range(16):
                gath[g, j, y, x, :, b * 128 : (b + 1) * 128] = v[b * 16 : (b + 1) * 16]

        keep(0, g_y * z_val)
        keep(1, du * value)
        keep(2, du * key)
        out = (gate * z_val).astype(BF16)
        for b in range(16):
            bo0[b // 4, g, b % 4] = out[b * 16 : (b + 1) * 16]

        def sums():
            flip = (lax.broadcasted_iota(jnp.int32, (128, 128), 0) + lax.broadcasted_iota(jnp.int32, (128, 128), 1)) == 127
            dz_back = dot_nt(jnp.where(flip, 1.0, 0.0).astype(F32), dz, HIGHEST)
            lagged = pltpu.roll(dot_nn(dz_back, u_ext, HIGHEST), 129, 1, stride=1, stride_axis=0)
            by_lag = jnp.broadcast_to(jnp.sum(lagged, axis=0, keepdims=True), (8, 256))
            lag_rows = lax.broadcasted_iota(jnp.int32, (256, 128), 0)
            lag_cols = lax.broadcasted_iota(jnp.int32, (256, 128), 1)
            pick = jnp.where(lag_rows + lag_cols == 128, 1.0, 0.0).astype(F32)
            sm[y, x, g : g + 1, :] = dot_nn(by_lag, pick, HIGHEST)[:1] * scale
            product = dz * u
            folded = product[:16]
            for b in range(1, 16):
                folded = folded + product[b * 16 : (b + 1) * 16]
            per_ch = jnp.sum(folded, axis=1, keepdims=True) * scale
            placed = jnp.sum(jnp.where(mine, jnp.broadcast_to(per_ch, (16, 512)), 0.0), axis=0, keepdims=True)
            for i in range(2):
                o = g * 256 + i * 128
                sm[y, x, 4 + g * 2 + i : 5 + g * 2 + i, :] = placed[:, o : o + 128]

        return sums

    u1, u2, v1, v2 = {}, {}, {}, {}

    def ag_send(table, key, g, h, q_big, q_small, start, size, device):
        ref = one(gath, g, h, q_big, q_small, start, size)
        table[key] = send(ref, ref, device)

    def ag_open(g):
        for h in range(2):
            for d in range(2):
                ag_send(u1, (g, h, d), g, h, pos_big[h], pos_small[h], 0, 1024, small_dev[h](BY[d]))
        for h in range(2):
            for d in range(2):
                ag_send(v1, (g, h, 0, d), g, h, pos_big[h], pos_small[h], 0, 1024, big_dev[h](BY[d]))

    def ag_near(g):
        for h in range(2):
            for d in range(2):
                u1[g, h, d].wait_recv()
                ag_send(u2, (g, h, d), g, h, pos_big[h], m4(pos_small[h] - BY[d]), FAR[d], QUARTER, small_dev[h](BY[d]))
        for h in range(2):
            for e in range(2):
                for d in range(2):
                    ag_send(v1, (g, h, 1 + e, d), g, h, pos_big[h], m4(pos_small[h] - BY[e]), 0, 1024, big_dev[h](BY[d]))

    def ag_far(g):
        for h in range(2):
            for d in range(2):
                u2[g, h, d].wait_recv()
            for d in range(2):
                ag_send(v1, (g, h, 3, d), g, h, pos_big[h], m4(pos_small[h] + 2), 0, 1024, big_dev[h](BY[d]))

    def ag_forward(g, piece):
        for h in range(2):
            q = m4(pos_small[h] + (0, -1, 1, 2)[piece])
            for d in range(2):
                v1[g, h, piece, d].wait_recv()
                ag_send(v2, (g, h, piece, d), g, h, m4(pos_big[h] - BY[d]), q, FAR[d], QUARTER, big_dev[h](BY[d]))

    def ag_close(g):
        for h in range(2):
            for piece in range(4):
                for d in range(2):
                    v2[g, h, piece, d].wait_recv()

    def bo_first():
        bo1[y] = bo0[y]
        return [send(bo0.at[m4(y + k)], bo1.at[y], at_y(k)) for k in (1, -1, 2)]

    def bo_second(arriving):
        for copy in arriving:
            copy.wait_recv()
        bo2[x] = bo1[:, :, x]
        return [send(bo1.at[:, :, m4(x + k)], bo2.at[x], at_x(k)) for k in (1, -1, 2)]

    def bo_last(arriving):
        for copy in arriving:
            copy.wait_recv()
        for g in range(2):
            rows = jnp.concatenate([bo2[d % 4, d // 4, g] for d in range(16)], axis=0)
            bo_out[:, g * 256 : (g + 1) * 256] = rows.T

    gy_t = gy[...].T
    for g in range(2):
        for d in range(16):
            gyt[d % 4, d // 4, g] = gy_t[g * 256 + d * 16 : g * 256 + (d + 1) * 16]
    gy1[x] = gyt[x]
    sm[y, x] = jnp.zeros((8, 128), F32)
    w_load[0].wait()
    transpose_w(0)
    pl.semaphore_wait(barrier, len(partners))
    gy_a = [send(gyt.at[m4(x + k)], gy1.at[x], at_x(k)) for k in (1, -1, 2)]
    for i in range(4):
        bi_load[i].wait()
        project_rows(0, quarter[i])
        send_s1_one(0, i // 2, i % 2)
    send_s2a(0)
    w_load[1].wait()
    transpose_w(1)
    for copy in gy_a:
        copy.wait_recv()
    gy2[y] = gy1[:, y]
    gy_b = [send(gy1.at[:, m4(y + k)], gy2.at[y], at_y(k)) for k in (1, -1, 2)]
    project(1)
    send_s2b(0)
    send_s1(1)
    transpose_bi()
    finish_big(0)
    send_s2a(1)
    send_t2b(0)
    send_s2b(1)
    for copy in gy_b:
        copy.wait_recv()
    sums0 = filter_group(0)
    ag_open(0)
    sums0()
    finish_big(1)
    ag_near(0)
    send_t2b(1)
    ag_forward(0, 0)
    ag_far(0)
    sums1 = filter_group(1)
    ag_open(1)
    sums1()
    ag_forward(0, 1)
    ag_forward(0, 2)
    ag_near(1)
    ag_forward(0, 3)
    ag_far(1)
    ag_close(0)
    ag_forward(1, 0)
    sm_a = [send(sm.at[y, x], sm.at[y, x], at_y(k)) for k in (1, -1, 2)]
    grad_x_near(0)
    grad_x_near(1)
    ag_forward(1, 1)
    ag_forward(1, 2)
    grad_x_near(2)
    grad_x_near(3)
    for copy in sm_a:
        copy.wait_recv()
    sm_b = [send(sm.at[:, x], sm.at[:, x], at_x(k)) for k in (1, -1, 2)]
    ag_forward(1, 3)
    for j in range(3):
        for i in range(2):
            grad_w(0, j, i)
    ag_close(1)

    order = (4, 3, -3, 2, -2, 1, -1, 0)
    pair, ring = {}, {}
    FARZ, NEARZ = (0, 256), (256, 0)

    def pair_send(k):
        q = m8(z + k)
        grad_x_chunk(q)
        theirs = pl.ds(pl.multiple_of((q * 2 + (1 - core)) * 128, 128), 128)
        cs[q] = gx[:, theirs].astype(BF16)
        pair[k] = send(cs.at[q], cr.at[q], at_core)

    def pair_sum(k):
        q = m8(z + k)
        own = pl.ds(pl.multiple_of((q * 2 + core) * 128, 128), 128)
        pair[k].wait_recv()
        zs[q] = (gx[:, own] + cr[q].astype(F32)).astype(BF16)

    def z_send(d, k, far):
        q = m8(z + BY[d] * k)
        first = k == (4 if far else 3)
        slot = (4 - k) if far else (4 + 3 - k)
        for i in range(2):
            r = (FARZ if far else NEARZ)[d] + i * 128
            rows = slice(r, r + 128)
            if not first:
                ring[d, k + 1, far, i].wait_recv()
                came = zr[d, slot - 1, i * 128 : (i + 1) * 128]
                zs[q, rows] = (zs[q, rows].astype(F32) + came.astype(F32)).astype(BF16)
            ring[d, k, far, i] = send(zs.at[q, pl.ds(r, 128)], zr.at[d, slot, pl.ds(i * 128, 128)], at_z(BY[d]))

    def z_both(k, far):
        for d in range(2):
            z_send(d, k, far)

    pair_send(4)
    pair_send(3)
    pair_send(-3)
    pair_sum(4)
    z_both(4, True)
    pair_sum(3)
    pair_sum(-3)
    z_both(3, False)
    pair_send(2)
    pair_send(-2)
    z_both(3, True)
    pair_sum(2)
    pair_sum(-2)
    bo_a = bo_first()
    pair_send(1)
    pair_send(-1)
    z_both(2, False)
    pair_sum(1)
    pair_sum(-1)
    pair_send(0)
    z_both(2, True)
    grad_w(1, 0, 0)
    grad_w(1, 0, 1)
    z_both(1, False)
    pair_sum(0)
    bo_b = bo_second(bo_a)
    grad_w(1, 1, 0)
    z_both(1, True)
    grad_w(1, 1, 1)
    grad_w(1, 2, 0)
    grad_w(1, 2, 1)
    for copy in sm_b:
        copy.wait_recv()
    for g in range(2):
        for d in range(16):
            gf_out[g * 16 + d : g * 16 + d + 1, :] = sm[d // 4, d % 4, g : g + 1, :]
    skips = sm[0, 0, 4:8, :]
    for d in range(1, 16):
        skips = skips + sm[d // 4, d % 4, 4:8, :]
    gs_out[...] = skips
    bo_last(bo_b)

    for far in (False, True):
        for d in range(2):
            for i in range(2):
                ring[d, 1, far, i].wait_recv()
    own = zs[z]
    top = own[:256].astype(F32) + zr[0, 3].astype(F32) + zr[1, 6].astype(F32)
    low = own[256:].astype(F32) + zr[1, 3].astype(F32) + zr[0, 6].astype(F32)
    gx_out[:, :256] = top.T.astype(BF16)
    gx_out[:, 256:] = low.T.astype(BF16)
    for copy in sent:
        copy.wait_send()


def hand_on(*refs):
    came, out, sems = refs[:5], refs[5:10], refs[10]
    copies = [pltpu.make_async_copy(came[i], out[i], sems.at[i]) for i in range(5)]
    for copy in copies:
        copy.start()
    for copy in copies:
        copy.wait()


def per_device(block_in, w_in, filt, skip, grad_y):
    tokens = block_in.shape[0]
    scale = tokens ** (-0.5)
    vmem = pl.BlockSpec(memory_space=pltpu.VMEM)
    hbm = pl.BlockSpec(memory_space=pltpu.HBM)
    out_shape = (
        jax.ShapeDtypeStruct((128, 512), BF16),
        jax.ShapeDtypeStruct((128, 512), BF16),
        jax.ShapeDtypeStruct((3, 512, 512), F32),
        jax.ShapeDtypeStruct((32, 128), F32),
        jax.ShapeDtypeStruct((4, 128), F32),
    )
    scratch = [
        pltpu.VMEM((2048, 512), BF16),
        pltpu.VMEM((3, 512, 512), BF16),
        pltpu.VMEM((3, 512, 512), BF16),
        pltpu.VMEM((512, 2048), BF16),
        pltpu.VMEM((2, 3, 4, 4, 16, 2048), BF16),
        pltpu.VMEM((2, 2, 2, 3, 3, 4, 16, QUARTER), BF16),
        pltpu.VMEM((2, 2, 2, 3, 3, 16, QUARTER), BF16),
        pltpu.VMEM((2, 3, 4, 4, 16, 2048), BF16),
        pltpu.VMEM((512, 2048), F32),
        pltpu.VMEM((4, 4, 2, 16, 128), BF16),
        pltpu.VMEM((4, 4, 2, 16, 128), BF16),
        pltpu.VMEM((4, 4, 2, 16, 128), BF16),
        pltpu.VMEM((4, 2, 4, 16, 128), BF16),
        pltpu.VMEM((4, 2, 4, 16, 128), BF16),
        pltpu.VMEM((4, 4, 2, 16, 128), BF16),
        pltpu.VMEM((4, 4, 8, 128), F32),
        pltpu.VMEM((8, 512, 128), BF16),
        pltpu.VMEM((8, 512, 128), BF16),
        pltpu.VMEM((8, 512, 128), BF16),
        pltpu.VMEM((2, 7, 256, 128), BF16),
        pltpu.SemaphoreType.DMA((N_SEMS,)),
        pltpu.SemaphoreType.DMA((N_SEMS,)),
        pltpu.SemaphoreType.DMA((6,)),
    ]
    results = pl.pallas_call(
        functools.partial(block_kernel, scale),
        out_shape=out_shape,
        in_specs=[hbm, hbm, vmem, vmem, vmem],
        out_specs=[vmem] * 5,
        scratch_shapes=scratch,
        compiler_params=pltpu.CompilerParams(
            collective_id=0, has_side_effects=True, vmem_limit_bytes=44 * 2**20
        ),
        cost_estimate=pl.CostEstimate(flops=10**10, bytes_accessed=10**7, transcendentals=0),
    )(*(pltpu.with_memory_space_constraint(a, pltpu.HBM) for a in (block_in, w_in, filt, skip.reshape(1, 512), grad_y)))
    block_out, grad_x, grad_w, grad_filt, grad_skip = pl.pallas_call(
        hand_on,
        out_shape=out_shape,
        in_specs=[vmem] * 5,
        out_specs=[pl.BlockSpec(memory_space=pl.ANY)] * 5,
        scratch_shapes=[pltpu.SemaphoreType.DMA((5,))],
        compiler_params=pltpu.CompilerParams(vmem_limit_bytes=8 * 2**20),
    )(*results)
    return block_out, grad_x, grad_w, grad_filt, grad_skip.reshape(512)


def solution(mesh):
    in_specs = (P(None, "seq"), P(None, "seq", "tp"), P("tp", None), P("tp"), P("seq", "tp"))
    out_specs = (P("seq", "tp"), P("tp", "seq"), P(None, "seq", "tp"), P("tp", None), P("tp"))
    return jax.shard_map(per_device, mesh=mesh, in_specs=in_specs, out_specs=out_specs, check_vma=False)
```

```python
import functools

import jax
import jax.numpy as jnp
from jax import lax
from jax.experimental import pallas as pl
from jax.experimental.pallas import tpu as pltpu
from jax.sharding import PartitionSpec as P

MESH = pl.DeviceIdType.MESH
F32 = jnp.float32
BF16 = jnp.bfloat16
HIGHEST = lax.Precision.HIGHEST
N_SEMS = 256
QUARTER = 512


def dot_nt(a, b, precision=None):
    return lax.dot_general(a, b, (((1,), (1,)), ((), ())), precision=precision, preferred_element_type=F32)


def dot_nn(a, b, precision=None):
    return lax.dot_general(a, b, (((1,), (0,)), ((), ())), precision=precision, preferred_element_type=F32)


def block_kernel(
    scale, bi_in, w_in, filt_in, skip_in, gy_in, bo_out, gx_out, gw_out, gf_out, gs_out,
    bi, w, filt, skip, gy, wt, bit, part, r1, r2, gath, gx, gyt, gy1, gy2, bo0, bo1, bo2, sm, cs, cr, zs, zr, ssem, rsem, lsem,
):
    seq, tp = lax.axis_index("seq"), lax.axis_index("tp")
    x, y, z, core = lax.rem(seq, 4), lax.div(seq, 4), lax.div(tp, 2), lax.rem(tp, 2)

    def m4(v):
        return lax.rem(v + 4, 4)

    def m8(v):
        return lax.rem(v + 8, 8)

    def at_x(by):
        return (y * 4 + m4(x + by), tp)

    def at_y(by):
        return (m4(y + by) * 4 + x, tp)

    def at_z(by):
        return (seq, m8(z + by) * 2 + core)

    at_core = (seq, z * 2 + (1 - core))
    partners = [at_x(1), at_x(-1), at_x(2), at_y(1), at_y(-1), at_y(2), at_z(1), at_z(-1), at_core]

    barrier = pltpu.get_barrier_semaphore()
    for device in partners:
        pl.semaphore_signal(barrier, inc=1, device_id=device, device_id_type=MESH)

    def load(src, dst, k):
        copy = pltpu.make_async_copy(src, dst, lsem.at[k])
        copy.start()
        return copy

    half_w = [pl.ds(0, 256), pl.ds(256, 256)]
    quarter = [pl.ds(i * QUARTER, QUARTER) for i in range(4)]
    small_load = [load(gy_in, gy, 6), load(filt_in, filt, 7), load(skip_in, skip, 8)]
    w_load = [load(w_in.at[:, :, half_w[0]], w.at[:, :, half_w[0]], 0)]
    bi_load = [load(bi_in.at[q], bi.at[q], 2 + i) for i, q in enumerate(quarter)]
    w_load.append(load(w_in.at[:, :, half_w[1]], w.at[:, :, half_w[1]], 1))

    sent = []

    def send(src, dst, device):
        k = len(sent)
        copy = pltpu.make_async_remote_copy(
            src_ref=src, dst_ref=dst, send_sem=ssem.at[k], recv_sem=rsem.at[k], device_id=device, device_id_type=MESH
        )
        copy.start()
        sent.append(copy)
        return copy

    def transpose_w(g):
        for j in range(3):
            wt[j, g * 256 : (g + 1) * 256, :] = w[j, :, g * 256 : (g + 1) * 256].T

    def transpose_bi():
        @pl.loop(0, 4)
        def _(i):
            rows = pl.ds(pl.multiple_of(i * 512, 512), 512)
            bit[:, rows] = bi[rows, :].T

    def project_rows(g, rows):
        tokens = bi[rows, :]
        for j in range(3):
            p = dot_nt(wt[j, g * 256 : (g + 1) * 256, :], tokens).astype(BF16)
            part[g, j, :, :, :, rows] = p.reshape(4, 4, 16, 512)

    def project(g):
        @pl.loop(0, 4)
        def _(i):
            project_rows(g, pl.ds(pl.multiple_of(i * 512, 512), 512))

    def grad_x_near(i):
        rows = quarter[i]
        total = None
        for j in range(3):
            p = dot_nn(w[j, :, :256], gath[0, j, :, :, :, rows].reshape(256, QUARTER))
            total = p if total is None else total + p
        gx[:, rows] = total

    def grad_x_chunk(q):
        rows = pl.ds(pl.multiple_of(q * 256, 256), 256)
        total = gx[:, rows]
        for j in range(3):
            total = total + dot_nn(w[j, :, 256:], gath[1, j, :, :, :, rows].reshape(256, 256))
        gx[:, rows] = total

    def grad_w(g, j, i):
        d = gath[g, j].reshape(256, 2048)
        gw_out[j, i * 256 : (i + 1) * 256, half_w[g]] = dot_nt(bit[i * 256 : (i + 1) * 256, :], d) * scale

    pos_big, pos_small = (x, y), (y, x)
    big_dev, small_dev = (at_x, at_y), (at_y, at_x)

    def big(ref, g, h, q, start, size):
        tokens = pl.ds(h * 1024 + start, size)
        return ref.at[g, :, :, q, :, tokens] if h == 0 else ref.at[g, :, q, :, :, tokens]

    def one(ref, g, h, q_big, q_small, start, size):
        tokens = pl.ds(h * 1024 + start, size)
        return ref.at[g, :, q_small, q_big, :, tokens] if h == 0 else ref.at[g, :, q_big, q_small, :, tokens]

    def small(g, h, q, start, size):
        return one(part, g, h, pos_big[h], q, start, size)

    BY = (1, -1)
    FAR = (0, QUARTER)
    NEAR = (QUARTER, 0)

    def add_big(dst, *srcs):
        @pl.loop(0, 3)
        def _(j):
            for i in range(4):
                total = dst[j, i].astype(F32)
                for s in srcs:
                    total = total + s[j, i].astype(F32)
                dst[j, i] = total.astype(BF16)

    def add_small(dst, *srcs):
        for j in range(3):
            total = dst[j].astype(F32)
            for s in srcs:
                total = total + s[j].astype(F32)
            dst[j] = total.astype(BF16)

    s1, s2a, s2b, t1, t2a, t2b = {}, {}, {}, {}, {}, {}

    def send_s1_one(g, h, d):
        src = big(part, g, h, m4(pos_big[h] + 2), FAR[d], QUARTER)
        s1[g, h, d] = send(src, r1.at[g, h, d, 0], big_dev[h](BY[d]))

    def send_s1(g):
        for h in range(2):
            for d in range(2):
                send_s1_one(g, h, d)

    def send_s2a(g):
        for h in range(2):
            for d in range(2):
                src = big(part, g, h, m4(pos_big[h] + BY[d]), NEAR[d], QUARTER)
                s2a[g, h, d] = send(src, r1.at[g, h, d, 1], big_dev[h](BY[d]))

    def send_s2b(g):
        for h in range(2):
            for d in range(2):
                src = big(part, g, h, m4(pos_big[h] + BY[d]), FAR[d], QUARTER)
                s1[g, h, d].wait_recv()
                add_big(src, r1.at[g, h, d, 0])
                s2b[g, h, d] = send(src, r1.at[g, h, d, 2], big_dev[h](BY[d]))

    def finish_big(g):
        for h in range(2):
            for d in range(2):
                s2a[g, h, d].wait_recv()
        for h in range(2):
            for d in range(2):
                s2b[g, h, d].wait_recv()
                add_big(big(part, g, h, pos_big[h], FAR[d], QUARTER), r1.at[g, h, d, 2], r1.at[g, h, 1 - d, 1])
                t1[g, h, d] = send(small(g, h, m4(pos_small[h] + 2), FAR[d], QUARTER), r2.at[g, h, d, 0], small_dev[h](BY[d]))
                src = small(g, h, m4(pos_small[h] + BY[1 - d]), FAR[d], QUARTER)
                t2a[g, h, 1 - d] = send(src, r2.at[g, h, 1 - d, 1], small_dev[h](BY[1 - d]))

    def send_t2b(g):
        for h in range(2):
            for d in range(2):
                t1[g, h, d].wait_recv()
                src = small(g, h, m4(pos_small[h] + BY[d]), FAR[d], QUARTER)
                add_small(src, r2.at[g, h, d, 0])
                t2b[g, h, d] = send(src, r2.at[g, h, d, 2], small_dev[h](BY[d]))

    def filter_group(g):
        for h in range(2):
            for d in range(2):
                t2a[g, h, d].wait_recv()
                t2b[g, h, d].wait_recv()

        def stacked(j):
            pieces = []
            for b in range(16):
                h, d, o = b // 8, (b % 8) // 4, (b % 4) * 128
                total = part[g, j, y, x, :, b * 128 : (b + 1) * 128].astype(F32)
                total = total + r2[g, h, d, 2, j, :, o : o + 128].astype(F32)
                total = total + r2[g, h, 1 - d, 1, j, :, o : o + 128].astype(F32)
                pieces.append(total.astype(BF16).astype(F32))
            return jnp.concatenate(pieces, axis=0)

        gate, key, value = stacked(0), stacked(1), stacked(2)
        u = key * value
        blank = jnp.zeros((16, 128), F32)
        u_ext = jnp.concatenate([jnp.concatenate([blank, u[:240]], axis=0), u], axis=1)
        taps = jnp.broadcast_to(filt[pl.ds(g * 16 + seq, 1), :], (256, 128))
        taps = jnp.concatenate([taps, jnp.zeros((256, 128), F32)], axis=1)
        causal = pltpu.roll(taps, 128, 1, stride=1, stride_axis=0)[:, :128]
        anti = pltpu.roll(taps[:128], 0, 1, stride=1, stride_axis=0)

        lane = lax.broadcasted_iota(jnp.int32, (16, 512), 1)
        row = lax.broadcasted_iota(jnp.int32, (16, 512), 0)
        mine = lane == row + (g * 256 + seq * 16)
        skip_col = jnp.sum(jnp.where(mine, jnp.broadcast_to(skip[...], (16, 512)), 0.0), axis=1, keepdims=True)
        skip_all = jnp.concatenate([jnp.broadcast_to(skip_col, (16, 128))] * 16, axis=0)

        z_val = dot_nn(u_ext, causal, HIGHEST) + skip_all * u
        g_y = jnp.concatenate([gy2[b // 4, b % 4, g] for b in range(16)], axis=0).astype(F32)
        dz = g_y * gate
        dz_ext = jnp.concatenate([dz, jnp.concatenate([dz[16:], blank], axis=0)], axis=1)
        du = dot_nt(dz_ext, anti, HIGHEST) + skip_all * dz

        def keep(j, value_of):
            v = value_of.astype(BF16)
            for b in range(16):
                gath[g, j, y, x, :, b * 128 : (b + 1) * 128] = v[b * 16 : (b + 1) * 16]

        keep(0, g_y * z_val)
        keep(1, du * value)
        keep(2, du * key)
        out = (gate * z_val).astype(BF16)
        for b in range(16):
            bo0[b // 4, g, b % 4] = out[b * 16 : (b + 1) * 16]

        def sums():
            flip = (lax.broadcasted_iota(jnp.int32, (128, 128), 0) + lax.broadcasted_iota(jnp.int32, (128, 128), 1)) == 127
            dz_back = dot_nt(jnp.where(flip, 1.0, 0.0).astype(F32), dz, HIGHEST)
            lagged = pltpu.roll(dot_nn(dz_back, u_ext, HIGHEST), 129, 1, stride=1, stride_axis=0)
            by_lag = jnp.broadcast_to(jnp.sum(lagged, axis=0, keepdims=True), (8, 256))
            lag_rows = lax.broadcasted_iota(jnp.int32, (256, 128), 0)
            lag_cols = lax.broadcasted_iota(jnp.int32, (256, 128), 1)
            pick = jnp.where(lag_rows + lag_cols == 128, 1.0, 0.0).astype(F32)
            sm[y, x, g : g + 1, :] = dot_nn(by_lag, pick, HIGHEST)[:1] * scale
            product = dz * u
            folded = product[:16]
            for b in range(1, 16):
                folded = folded + product[b * 16 : (b + 1) * 16]
            per_ch = jnp.sum(folded, axis=1, keepdims=True) * scale
            placed = jnp.sum(jnp.where(mine, jnp.broadcast_to(per_ch, (16, 512)), 0.0), axis=0, keepdims=True)
            for i in range(2):
                o = g * 256 + i * 128
                sm[y, x, 4 + g * 2 + i : 5 + g * 2 + i, :] = placed[:, o : o + 128]

        return sums

    u1, u2, v1, v2 = {}, {}, {}, {}

    def ag_send(table, key, g, h, q_big, q_small, start, size, device):
        ref = one(gath, g, h, q_big, q_small, start, size)
        table[key] = send(ref, ref, device)

    def ag_open(g):
        for h in range(2):
            for d in range(2):
                ag_send(u1, (g, h, d), g, h, pos_big[h], pos_small[h], 0, 1024, small_dev[h](BY[d]))
        for h in range(2):
            for d in range(2):
                ag_send(v1, (g, h, 0, d), g, h, pos_big[h], pos_small[h], 0, 1024, big_dev[h](BY[d]))

    def ag_near(g):
        for h in range(2):
            for d in range(2):
                u1[g, h, d].wait_recv()
                ag_send(u2, (g, h, d), g, h, pos_big[h], m4(pos_small[h] - BY[d]), FAR[d], QUARTER, small_dev[h](BY[d]))
        for h in range(2):
            for e in range(2):
                for d in range(2):
                    ag_send(v1, (g, h, 1 + e, d), g, h, pos_big[h], m4(pos_small[h] - BY[e]), 0, 1024, big_dev[h](BY[d]))

    def ag_far(g):
        for h in range(2):
            for d in range(2):
                u2[g, h, d].wait_recv()
            for d in range(2):
                ag_send(v1, (g, h, 3, d), g, h, pos_big[h], m4(pos_small[h] + 2), 0, 1024, big_dev[h](BY[d]))

    def ag_forward(g, piece):
        for h in range(2):
            q = m4(pos_small[h] + (0, -1, 1, 2)[piece])
            for d in range(2):
                v1[g, h, piece, d].wait_recv()
                ag_send(v2, (g, h, piece, d), g, h, m4(pos_big[h] - BY[d]), q, FAR[d], QUARTER, big_dev[h](BY[d]))

    def ag_close(g):
        for h in range(2):
            for piece in range(4):
                for d in range(2):
                    v2[g, h, piece, d].wait_recv()

    def bo_first():
        bo1[y] = bo0[y]
        return [send(bo0.at[m4(y + k)], bo1.at[y], at_y(k)) for k in (1, -1, 2)]

    def bo_second(arriving):
        for copy in arriving:
            copy.wait_recv()
        bo2[x] = bo1[:, :, x]
        return [send(bo1.at[:, :, m4(x + k)], bo2.at[x], at_x(k)) for k in (1, -1, 2)]

    def bo_last(arriving):
        for copy in arriving:
            copy.wait_recv()
        for g in range(2):
            rows = jnp.concatenate([bo2[d % 4, d // 4, g] for d in range(16)], axis=0)
            bo_out[:, g * 256 : (g + 1) * 256] = rows.T

    for copy in small_load:
        copy.wait()
    gy_t = gy[...].T
    for g in range(2):
        for d in range(16):
            gyt[d % 4, d // 4, g] = gy_t[g * 256 + d * 16 : g * 256 + (d + 1) * 16]
    gy1[x] = gyt[x]
    sm[y, x] = jnp.zeros((8, 128), F32)
    pl.semaphore_wait(barrier, len(partners))
    gy_a = [send(gyt.at[m4(x + k)], gy1.at[x], at_x(k)) for k in (1, -1, 2)]
    w_load[0].wait()
    transpose_w(0)
    for i in range(4):
        bi_load[i].wait()
        project_rows(0, quarter[i])
        send_s1_one(0, i // 2, i % 2)
    send_s2a(0)
    w_load[1].wait()
    transpose_w(1)
    for copy in gy_a:
        copy.wait_recv()
    gy2[y] = gy1[:, y]
    gy_b = [send(gy1.at[:, m4(y + k)], gy2.at[y], at_y(k)) for k in (1, -1, 2)]
    project(1)
    send_s2b(0)
    send_s1(1)
    transpose_bi()
    finish_big(0)
    send_s2a(1)
    send_t2b(0)
    send_s2b(1)
    for copy in gy_b:
        copy.wait_recv()
    sums0 = filter_group(0)
    ag_open(0)
    sums0()
    finish_big(1)
    ag_near(0)
    send_t2b(1)
    ag_forward(0, 0)
    ag_far(0)
    sums1 = filter_group(1)
    ag_open(1)
    sums1()
    ag_forward(0, 1)
    ag_forward(0, 2)
    ag_near(1)
    ag_forward(0, 3)
    ag_far(1)
    ag_close(0)
    ag_forward(1, 0)
    sm_a = [send(sm.at[y, x], sm.at[y, x], at_y(k)) for k in (1, -1, 2)]
    grad_x_near(0)
    grad_x_near(1)
    grad_w(0, 0, 0)
    grad_w(0, 0, 1)
    ag_forward(1, 1)
    ag_forward(1, 2)
    grad_w(0, 1, 0)
    grad_w(0, 1, 1)
    grad_x_near(2)
    grad_x_near(3)
    grad_w(0, 2, 0)
    grad_w(0, 2, 1)
    for copy in sm_a:
        copy.wait_recv()
    sm_b = [send(sm.at[:, x], sm.at[:, x], at_x(k)) for k in (1, -1, 2)]
    ag_forward(1, 3)
    ag_close(1)

    order = (4, 3, -3, 2, -2, 1, -1, 0)
    pair, ring = {}, {}
    FARZ, NEARZ = (0, 256), (256, 0)

    def pair_send(k):
        q = m8(z + k)
        grad_x_chunk(q)
        theirs = pl.ds(pl.multiple_of((q * 2 + (1 - core)) * 128, 128), 128)
        cs[q] = gx[:, theirs].astype(BF16)
        pair[k] = send(cs.at[q], cr.at[q], at_core)

    def pair_sum(k):
        q = m8(z + k)
        own = pl.ds(pl.multiple_of((q * 2 + core) * 128, 128), 128)
        pair[k].wait_recv()
        zs[q] = (gx[:, own] + cr[q].astype(F32)).astype(BF16)

    def z_send(d, k, far):
        q = m8(z + BY[d] * k)
        first = k == (4 if far else 3)
        slot = (4 - k) if far else (4 + 3 - k)
        for i in range(2):
            r = (FARZ if far else NEARZ)[d] + i * 128
            rows = slice(r, r + 128)
            if not first:
                ring[d, k + 1, far, i].wait_recv()
                came = zr[d, slot - 1, i * 128 : (i + 1) * 128]
                zs[q, rows] = (zs[q, rows].astype(F32) + came.astype(F32)).astype(BF16)
            ring[d, k, far, i] = send(zs.at[q, pl.ds(r, 128)], zr.at[d, slot, pl.ds(i * 128, 128)], at_z(BY[d]))

    def z_both(k, far):
        for d in range(2):
            z_send(d, k, far)

    pair_send(4)
    pair_send(3)
    pair_sum(4)
    z_both(4, True)
    pair_send(-3)
    pair_sum(3)
    z_send(0, 3, False)
    pair_sum(-3)
    z_send(1, 3, False)
    pair_send(2)
    pair_send(-2)
    z_both(3, True)
    pair_sum(2)
    pair_sum(-2)
    bo_a = bo_first()
    pair_send(1)
    pair_send(-1)
    z_both(2, False)
    pair_sum(1)
    pair_sum(-1)
    pair_send(0)
    z_both(2, True)
    grad_w(1, 0, 0)
    grad_w(1, 0, 1)
    z_both(1, False)
    pair_sum(0)
    bo_b = bo_second(bo_a)
    grad_w(1, 1, 0)
    z_both(1, True)
    grad_w(1, 1, 1)
    grad_w(1, 2, 0)
    grad_w(1, 2, 1)
    for copy in sm_b:
        copy.wait_recv()
    for g in range(2):
        for d in range(16):
            gf_out[g * 16 + d : g * 16 + d + 1, :] = sm[d // 4, d % 4, g : g + 1, :]
    skips = sm[0, 0, 4:8, :]
    for d in range(1, 16):
        skips = skips + sm[d // 4, d % 4, 4:8, :]
    gs_out[...] = skips
    bo_last(bo_b)

    for far in (False, True):
        for d in range(2):
            for i in range(2):
                ring[d, 1, far, i].wait_recv()
    own = zs[z]
    top = own[:256].astype(F32) + zr[0, 3].astype(F32) + zr[1, 6].astype(F32)
    low = own[256:].astype(F32) + zr[1, 3].astype(F32) + zr[0, 6].astype(F32)
    gx_out[:, :256] = top.T.astype(BF16)
    gx_out[:, 256:] = low.T.astype(BF16)
    for copy in sent:
        copy.wait_send()


def hand_on(*refs):
    came, out, sems = refs[:5], refs[5:10], refs[10]
    copies = [pltpu.make_async_copy(came[i], out[i], sems.at[i]) for i in range(5)]
    for copy in copies:
        copy.start()
    for copy in copies:
        copy.wait()


def per_device(block_in, w_in, filt, skip, grad_y):
    tokens = block_in.shape[0]
    scale = tokens ** (-0.5)
    vmem = pl.BlockSpec(memory_space=pltpu.VMEM)
    hbm = pl.BlockSpec(memory_space=pltpu.HBM)
    out_shape = (
        jax.ShapeDtypeStruct((128, 512), BF16),
        jax.ShapeDtypeStruct((128, 512), BF16),
        jax.ShapeDtypeStruct((3, 512, 512), F32),
        jax.ShapeDtypeStruct((32, 128), F32),
        jax.ShapeDtypeStruct((4, 128), F32),
    )
    scratch = [
        pltpu.VMEM((2048, 512), BF16),
        pltpu.VMEM((3, 512, 512), BF16),
        pltpu.VMEM((32, 128), F32),
        pltpu.VMEM((1, 512), F32),
        pltpu.VMEM((128, 512), BF16),
        pltpu.VMEM((3, 512, 512), BF16),
        pltpu.VMEM((512, 2048), BF16),
        pltpu.VMEM((2, 3, 4, 4, 16, 2048), BF16),
        pltpu.VMEM((2, 2, 2, 3, 3, 4, 16, QUARTER), BF16),
        pltpu.VMEM((2, 2, 2, 3, 3, 16, QUARTER), BF16),
        pltpu.VMEM((2, 3, 4, 4, 16, 2048), BF16),
        pltpu.VMEM((512, 2048), F32),
        pltpu.VMEM((4, 4, 2, 16, 128), BF16),
        pltpu.VMEM((4, 4, 2, 16, 128), BF16),
        pltpu.VMEM((4, 4, 2, 16, 128), BF16),
        pltpu.VMEM((4, 2, 4, 16, 128), BF16),
        pltpu.VMEM((4, 2, 4, 16, 128), BF16),
        pltpu.VMEM((4, 4, 2, 16, 128), BF16),
        pltpu.VMEM((4, 4, 8, 128), F32),
        pltpu.VMEM((8, 512, 128), BF16),
        pltpu.VMEM((8, 512, 128), BF16),
        pltpu.VMEM((8, 512, 128), BF16),
        pltpu.VMEM((2, 7, 256, 128), BF16),
        pltpu.SemaphoreType.DMA((N_SEMS,)),
        pltpu.SemaphoreType.DMA((N_SEMS,)),
        pltpu.SemaphoreType.DMA((9,)),
    ]
    results = pl.pallas_call(
        functools.partial(block_kernel, scale),
        out_shape=out_shape,
        in_specs=[hbm] * 5,
        out_specs=[vmem] * 5,
        scratch_shapes=scratch,
        compiler_params=pltpu.CompilerParams(
            collective_id=0, has_side_effects=True, vmem_limit_bytes=44 * 2**20
        ),
        cost_estimate=pl.CostEstimate(flops=10**10, bytes_accessed=10**7, transcendentals=0),
    )(*(pltpu.with_memory_space_constraint(a, pltpu.HBM) for a in (block_in, w_in, filt, skip.reshape(1, 512), grad_y)))
    block_out, grad_x, grad_w, grad_filt, grad_skip = pl.pallas_call(
        hand_on,
        out_shape=out_shape,
        in_specs=[vmem] * 5,
        out_specs=[pl.BlockSpec(memory_space=pl.ANY)] * 5,
        scratch_shapes=[pltpu.SemaphoreType.DMA((5,))],
        compiler_params=pltpu.CompilerParams(vmem_limit_bytes=8 * 2**20),
    )(*results)
    return block_out, grad_x, grad_w, grad_filt, grad_skip.reshape(512)


def solution(mesh):
    in_specs = (P(None, "seq"), P(None, "seq", "tp"), P("tp", None), P("tp"), P("seq", "tp"))
    out_specs = (P("seq", "tp"), P("tp", "seq"), P(None, "seq", "tp"), P("tp", None), P("tp"))
    return jax.shard_map(per_device, mesh=mesh, in_specs=in_specs, out_specs=out_specs, check_vma=False)
```

```python
import functools

import jax
import jax.numpy as jnp
from jax import lax
from jax.experimental import pallas as pl
from jax.experimental.pallas import tpu as pltpu
from jax.sharding import PartitionSpec as P

MESH = pl.DeviceIdType.MESH
F32 = jnp.float32
BF16 = jnp.bfloat16
HIGHEST = lax.Precision.HIGHEST
N_SEMS = 256
QUARTER = 512


def dot_nt(a, b, precision=None):
    return lax.dot_general(a, b, (((1,), (1,)), ((), ())), precision=precision, preferred_element_type=F32)


def dot_nn(a, b, precision=None):
    return lax.dot_general(a, b, (((1,), (0,)), ((), ())), precision=precision, preferred_element_type=F32)


def block_kernel(
    scale, bi_in, w_in, filt_in, skip_in, gy_in, bo_out, gx_out, gw_out, gf_out, gs_out,
    bi, w, filt, skip, gy, wt, bit, part, r1, r2, gath, gx, gyt, gy1, gy2, bo0, bo1, bo2, sm, cs, cr, zs, zr, ssem, rsem, lsem,
):
    seq, tp = lax.axis_index("seq"), lax.axis_index("tp")
    x, y, z, core = lax.rem(seq, 4), lax.div(seq, 4), lax.div(tp, 2), lax.rem(tp, 2)

    def m4(v):
        return lax.rem(v + 4, 4)

    def m8(v):
        return lax.rem(v + 8, 8)

    def at_x(by):
        return (y * 4 + m4(x + by), tp)

    def at_y(by):
        return (m4(y + by) * 4 + x, tp)

    def at_z(by):
        return (seq, m8(z + by) * 2 + core)

    at_core = (seq, z * 2 + (1 - core))
    partners = [at_x(1), at_x(-1), at_x(2), at_y(1), at_y(-1), at_y(2), at_z(1), at_z(-1), at_core]

    barrier = pltpu.get_barrier_semaphore()
    for device in partners:
        pl.semaphore_signal(barrier, inc=1, device_id=device, device_id_type=MESH)

    def load(src, dst, k):
        copy = pltpu.make_async_copy(src, dst, lsem.at[k])
        copy.start()
        return copy

    half_w = [pl.ds(0, 256), pl.ds(256, 256)]
    quarter = [pl.ds(i * QUARTER, QUARTER) for i in range(4)]
    small_load = [load(gy_in, gy, 6), load(filt_in, filt, 7), load(skip_in, skip, 8)]
    w_load = [load(w_in.at[:, :, half_w[0]], w.at[:, :, half_w[0]], 0)]
    bi_load = [load(bi_in.at[q], bi.at[q], 2 + i) for i, q in enumerate(quarter)]
    w_load.append(load(w_in.at[:, :, half_w[1]], w.at[:, :, half_w[1]], 1))

    sent = []

    def send(src, dst, device):
        k = len(sent)
        copy = pltpu.make_async_remote_copy(
            src_ref=src, dst_ref=dst, send_sem=ssem.at[k], recv_sem=rsem.at[k], device_id=device, device_id_type=MESH
        )
        copy.start()
        sent.append(copy)
        return copy

    def transpose_w(g):
        for j in range(3):
            wt[j, g * 256 : (g + 1) * 256, :] = w[j, :, g * 256 : (g + 1) * 256].T

    def transpose_bi():
        @pl.loop(0, 4)
        def _(i):
            rows = pl.ds(pl.multiple_of(i * 512, 512), 512)
            bit[:, rows] = bi[rows, :].T

    def project_rows(g, rows):
        tokens = bi[rows, :]
        for j in range(3):
            p = dot_nt(wt[j, g * 256 : (g + 1) * 256, :], tokens).astype(BF16)
            part[g, j, :, :, :, rows] = p.reshape(4, 4, 16, 512)

    def project(g):
        @pl.loop(0, 4)
        def _(i):
            project_rows(g, pl.ds(pl.multiple_of(i * 512, 512), 512))

    def grad_x_near(i):
        rows = quarter[i]
        total = None
        for j in range(3):
            p = dot_nn(w[j, :, :256], gath[0, j, :, :, :, rows].reshape(256, QUARTER))
            total = p if total is None else total + p
        gx[:, rows] = total

    def grad_x_chunk(q):
        rows = pl.ds(pl.multiple_of(q * 256, 256), 256)
        total = gx[:, rows]
        for j in range(3):
            total = total + dot_nn(w[j, :, 256:], gath[1, j, :, :, :, rows].reshape(256, 256))
        gx[:, rows] = total

    def grad_w(g, j, i):
        d = gath[g, j].reshape(256, 2048)
        gw_out[j, i * 256 : (i + 1) * 256, half_w[g]] = dot_nt(bit[i * 256 : (i + 1) * 256, :], d) * scale

    pos_big, pos_small = (x, y), (y, x)
    big_dev, small_dev = (at_x, at_y), (at_y, at_x)

    def big(ref, g, h, q, start, size):
        tokens = pl.ds(h * 1024 + start, size)
        return ref.at[g, :, :, q, :, tokens] if h == 0 else ref.at[g, :, q, :, :, tokens]

    def one(ref, g, h, q_big, q_small, start, size):
        tokens = pl.ds(h * 1024 + start, size)
        return ref.at[g, :, q_small, q_big, :, tokens] if h == 0 else ref.at[g, :, q_big, q_small, :, tokens]

    def small(g, h, q, start, size):
        return one(part, g, h, pos_big[h], q, start, size)

    BY = (1, -1)
    FAR = (0, QUARTER)
    NEAR = (QUARTER, 0)

    def add_big(dst, *srcs):
        @pl.loop(0, 3)
        def _(j):
            for i in range(4):
                total = dst[j, i].astype(F32)
                for s in srcs:
                    total = total + s[j, i].astype(F32)
                dst[j, i] = total.astype(BF16)

    def add_small(dst, *srcs):
        for j in range(3):
            total = dst[j].astype(F32)
            for s in srcs:
                total = total + s[j].astype(F32)
            dst[j] = total.astype(BF16)

    s1, s2a, s2b, t1, t2a, t2b = {}, {}, {}, {}, {}, {}

    def send_s1_one(g, h, d):
        src = big(part, g, h, m4(pos_big[h] + 2), FAR[d], QUARTER)
        s1[g, h, d] = send(src, r1.at[g, h, d, 0], big_dev[h](BY[d]))

    def send_s1(g):
        for h in range(2):
            for d in range(2):
                send_s1_one(g, h, d)

    def send_s2a(g):
        for h in range(2):
            for d in range(2):
                src = big(part, g, h, m4(pos_big[h] + BY[d]), NEAR[d], QUARTER)
                s2a[g, h, d] = send(src, r1.at[g, h, d, 1], big_dev[h](BY[d]))

    def send_s2b(g):
        for h in range(2):
            for d in range(2):
                src = big(part, g, h, m4(pos_big[h] + BY[d]), FAR[d], QUARTER)
                s1[g, h, d].wait_recv()
                add_big(src, r1.at[g, h, d, 0])
                s2b[g, h, d] = send(src, r1.at[g, h, d, 2], big_dev[h](BY[d]))

    def finish_big(g):
        for h in range(2):
            for d in range(2):
                s2a[g, h, d].wait_recv()
        for h in range(2):
            for d in range(2):
                s2b[g, h, d].wait_recv()
                add_big(big(part, g, h, pos_big[h], FAR[d], QUARTER), r1.at[g, h, d, 2], r1.at[g, h, 1 - d, 1])
                t1[g, h, d] = send(small(g, h, m4(pos_small[h] + 2), FAR[d], QUARTER), r2.at[g, h, d, 0], small_dev[h](BY[d]))
                src = small(g, h, m4(pos_small[h] + BY[1 - d]), FAR[d], QUARTER)
                t2a[g, h, 1 - d] = send(src, r2.at[g, h, 1 - d, 1], small_dev[h](BY[1 - d]))

    def send_t2b(g):
        for h in range(2):
            for d in range(2):
                t1[g, h, d].wait_recv()
                src = small(g, h, m4(pos_small[h] + BY[d]), FAR[d], QUARTER)
                add_small(src, r2.at[g, h, d, 0])
                t2b[g, h, d] = send(src, r2.at[g, h, d, 2], small_dev[h](BY[d]))

    def filter_group(g):
        for h in range(2):
            for d in range(2):
                t2a[g, h, d].wait_recv()
                t2b[g, h, d].wait_recv()

        def stacked(j):
            pieces = []
            for b in range(16):
                h, d, o = b // 8, (b % 8) // 4, (b % 4) * 128
                total = part[g, j, y, x, :, b * 128 : (b + 1) * 128].astype(F32)
                total = total + r2[g, h, d, 2, j, :, o : o + 128].astype(F32)
                total = total + r2[g, h, 1 - d, 1, j, :, o : o + 128].astype(F32)
                pieces.append(total.astype(BF16).astype(F32))
            return jnp.concatenate(pieces, axis=0)

        gate, key, value = stacked(0), stacked(1), stacked(2)
        u = key * value
        blank = jnp.zeros((16, 128), F32)
        u_ext = jnp.concatenate([jnp.concatenate([blank, u[:240]], axis=0), u], axis=1)
        taps = jnp.broadcast_to(filt[pl.ds(g * 16 + seq, 1), :], (256, 128))
        taps = jnp.concatenate([taps, jnp.zeros((256, 128), F32)], axis=1)
        causal = pltpu.roll(taps, 128, 1, stride=1, stride_axis=0)[:, :128]
        anti = pltpu.roll(taps[:128], 0, 1, stride=1, stride_axis=0)

        lane = lax.broadcasted_iota(jnp.int32, (16, 512), 1)
        row = lax.broadcasted_iota(jnp.int32, (16, 512), 0)
        mine = lane == row + (g * 256 + seq * 16)
        skip_col = jnp.sum(jnp.where(mine, jnp.broadcast_to(skip[...], (16, 512)), 0.0), axis=1, keepdims=True)
        skip_all = jnp.concatenate([jnp.broadcast_to(skip_col, (16, 128))] * 16, axis=0)

        z_val = dot_nn(u_ext, causal, HIGHEST) + skip_all * u
        g_y = jnp.concatenate([gy2[b // 4, b % 4, g] for b in range(16)], axis=0).astype(F32)
        dz = g_y * gate
        dz_ext = jnp.concatenate([dz, jnp.concatenate([dz[16:], blank], axis=0)], axis=1)
        du = dot_nt(dz_ext, anti, HIGHEST) + skip_all * dz

        def keep(j, value_of):
            v = value_of.astype(BF16)
            for b in range(16):
                gath[g, j, y, x, :, b * 128 : (b + 1) * 128] = v[b * 16 : (b + 1) * 16]

        keep(0, g_y * z_val)
        keep(1, du * value)
        keep(2, du * key)
        out = (gate * z_val).astype(BF16)
        for b in range(16):
            bo0[b // 4, g, b % 4] = out[b * 16 : (b + 1) * 16]

        def sums():
            flip = (lax.broadcasted_iota(jnp.int32, (128, 128), 0) + lax.broadcasted_iota(jnp.int32, (128, 128), 1)) == 127
            dz_back = dot_nt(jnp.where(flip, 1.0, 0.0).astype(F32), dz, HIGHEST)
            lagged = pltpu.roll(dot_nn(dz_back, u_ext, HIGHEST), 129, 1, stride=1, stride_axis=0)
            by_lag = jnp.broadcast_to(jnp.sum(lagged, axis=0, keepdims=True), (8, 256))
            lag_rows = lax.broadcasted_iota(jnp.int32, (256, 128), 0)
            lag_cols = lax.broadcasted_iota(jnp.int32, (256, 128), 1)
            pick = jnp.where(lag_rows + lag_cols == 128, 1.0, 0.0).astype(F32)
            sm[y, x, g : g + 1, :] = dot_nn(by_lag, pick, HIGHEST)[:1] * scale
            product = dz * u
            folded = product[:16]
            for b in range(1, 16):
                folded = folded + product[b * 16 : (b + 1) * 16]
            per_ch = jnp.sum(folded, axis=1, keepdims=True) * scale
            placed = jnp.sum(jnp.where(mine, jnp.broadcast_to(per_ch, (16, 512)), 0.0), axis=0, keepdims=True)
            for i in range(2):
                o = g * 256 + i * 128
                sm[y, x, 4 + g * 2 + i : 5 + g * 2 + i, :] = placed[:, o : o + 128]

        return sums

    u1, u2, v1, v2 = {}, {}, {}, {}

    def ag_send(table, key, g, h, q_big, q_small, start, size, device):
        ref = one(gath, g, h, q_big, q_small, start, size)
        table[key] = send(ref, ref, device)

    def ag_open(g):
        for h in range(2):
            for d in range(2):
                ag_send(u1, (g, h, d), g, h, pos_big[h], pos_small[h], 0, 1024, small_dev[h](BY[d]))
        for h in range(2):
            for d in range(2):
                ag_send(v1, (g, h, 0, d), g, h, pos_big[h], pos_small[h], 0, 1024, big_dev[h](BY[d]))

    def ag_near(g):
        for h in range(2):
            for d in range(2):
                u1[g, h, d].wait_recv()
                ag_send(u2, (g, h, d), g, h, pos_big[h], m4(pos_small[h] - BY[d]), FAR[d], QUARTER, small_dev[h](BY[d]))
        for h in range(2):
            for e in range(2):
                for d in range(2):
                    ag_send(v1, (g, h, 1 + e, d), g, h, pos_big[h], m4(pos_small[h] - BY[e]), 0, 1024, big_dev[h](BY[d]))

    def ag_far(g):
        for h in range(2):
            for d in range(2):
                u2[g, h, d].wait_recv()
            for d in range(2):
                ag_send(v1, (g, h, 3, d), g, h, pos_big[h], m4(pos_small[h] + 2), 0, 1024, big_dev[h](BY[d]))

    def ag_forward(g, piece):
        for h in range(2):
            q = m4(pos_small[h] + (0, -1, 1, 2)[piece])
            for d in range(2):
                v1[g, h, piece, d].wait_recv()
                ag_send(v2, (g, h, piece, d), g, h, m4(pos_big[h] - BY[d]), q, FAR[d], QUARTER, big_dev[h](BY[d]))

    def ag_close(g):
        for h in range(2):
            for piece in range(4):
                for d in range(2):
                    v2[g, h, piece, d].wait_recv()

    def bo_first():
        bo1[y] = bo0[y]
        return [send(bo0.at[m4(y + k)], bo1.at[y], at_y(k)) for k in (1, -1, 2)]

    def bo_second(arriving):
        for copy in arriving:
            copy.wait_recv()
        bo2[x] = bo1[:, :, x]
        return [send(bo1.at[:, :, m4(x + k)], bo2.at[x], at_x(k)) for k in (1, -1, 2)]

    def bo_last(arriving):
        for copy in arriving:
            copy.wait_recv()
        for g in range(2):
            rows = jnp.concatenate([bo2[d % 4, d // 4, g] for d in range(16)], axis=0)
            bo_out[:, g * 256 : (g + 1) * 256] = rows.T

    for copy in small_load:
        copy.wait()
    gy_t = gy[...].T
    for g in range(2):
        for d in range(16):
            gyt[d % 4, d // 4, g] = gy_t[g * 256 + d * 16 : g * 256 + (d + 1) * 16]
    gy1[0, x] = gyt[x, :, 0]
    gy1[1, y] = gyt[:, y, 1]
    sm[y, x] = jnp.zeros((8, 128), F32)
    pl.semaphore_wait(barrier, len(partners))
    gy_a = [send(gyt.at[m4(x + k), :, 0], gy1.at[0, x], at_x(k)) for k in (1, -1, 2)]
    gy_a += [send(gyt.at[:, m4(y + k), 1], gy1.at[1, y], at_y(k)) for k in (1, -1, 2)]
    w_load[0].wait()
    transpose_w(0)
    for i in range(4):
        bi_load[i].wait()
        project_rows(0, quarter[i])
        send_s1_one(0, i // 2, i % 2)
    send_s2a(0)
    w_load[1].wait()
    transpose_w(1)
    for copy in gy_a:
        copy.wait_recv()
    gy2[y, :, 0] = gy1[0, :, y]
    gy2[:, x, 1] = gy1[1, :, x]
    gy_b = [send(gy1.at[0, :, m4(y + k)], gy2.at[y, :, 0], at_y(k)) for k in (1, -1, 2)]
    gy_b += [send(gy1.at[1, :, m4(x + k)], gy2.at[:, x, 1], at_x(k)) for k in (1, -1, 2)]
    project(1)
    send_s2b(0)
    send_s1(1)
    transpose_bi()
    finish_big(0)
    send_s2a(1)
    send_t2b(0)
    send_s2b(1)
    for copy in gy_b:
        copy.wait_recv()
    sums0 = filter_group(0)
    ag_open(0)
    sums0()
    finish_big(1)
    ag_near(0)
    send_t2b(1)
    ag_forward(0, 0)
    ag_far(0)
    sums1 = filter_group(1)
    ag_open(1)
    sums1()
    ag_forward(0, 1)
    ag_forward(0, 2)
    ag_near(1)
    ag_forward(0, 3)
    ag_far(1)
    ag_close(0)
    ag_forward(1, 0)
    sm_a = [send(sm.at[y, x], sm.at[y, x], at_y(k)) for k in (1, -1, 2)]
    grad_x_near(0)
    grad_x_near(1)
    grad_w(0, 0, 0)
    grad_w(0, 0, 1)
    ag_forward(1, 1)
    ag_forward(1, 2)
    grad_w(0, 1, 0)
    grad_w(0, 1, 1)
    grad_x_near(2)
    grad_x_near(3)
    grad_w(0, 2, 0)
    grad_w(0, 2, 1)
    for copy in sm_a:
        copy.wait_recv()
    sm_b = [send(sm.at[:, x], sm.at[:, x], at_x(k)) for k in (1, -1, 2)]
    ag_forward(1, 3)
    ag_close(1)

    order = (4, 3, -3, 2, -2, 1, -1, 0)
    pair, ring = {}, {}
    FARZ, NEARZ = (0, 256), (256, 0)

    def pair_send(k):
        q = m8(z + k)
        grad_x_chunk(q)
        theirs = pl.ds(pl.multiple_of((q * 2 + (1 - core)) * 128, 128), 128)
        cs[q] = gx[:, theirs].astype(BF16)
        pair[k] = send(cs.at[q], cr.at[q], at_core)

    def pair_sum(k):
        q = m8(z + k)
        own = pl.ds(pl.multiple_of((q * 2 + core) * 128, 128), 128)
        pair[k].wait_recv()
        zs[q] = (gx[:, own] + cr[q].astype(F32)).astype(BF16)

    def z_send(d, k, far):
        q = m8(z + BY[d] * k)
        first = k == (4 if far else 3)
        slot = (4 - k) if far else (4 + 3 - k)
        for i in range(2):
            r = (FARZ if far else NEARZ)[d] + i * 128
            rows = slice(r, r + 128)
            if not first:
                ring[d, k + 1, far, i].wait_recv()
                came = zr[d, slot - 1, i * 128 : (i + 1) * 128]
                zs[q, rows] = (zs[q, rows].astype(F32) + came.astype(F32)).astype(BF16)
            ring[d, k, far, i] = send(zs.at[q, pl.ds(r, 128)], zr.at[d, slot, pl.ds(i * 128, 128)], at_z(BY[d]))

    def z_both(k, far):
        for d in range(2):
            z_send(d, k, far)

    pair_send(4)
    pair_send(3)
    pair_sum(4)
    z_both(4, True)
    pair_send(-3)
    pair_sum(3)
    z_send(0, 3, False)
    pair_sum(-3)
    z_send(1, 3, False)
    pair_send(2)
    pair_send(-2)
    z_both(3, True)
    pair_sum(2)
    pair_sum(-2)
    bo_a = bo_first()
    pair_send(1)
    pair_send(-1)
    z_both(2, False)
    pair_sum(1)
    pair_sum(-1)
    pair_send(0)
    z_both(2, True)
    grad_w(1, 0, 0)
    grad_w(1, 0, 1)
    z_both(1, False)
    pair_sum(0)
    bo_b = bo_second(bo_a)
    grad_w(1, 1, 0)
    z_both(1, True)
    grad_w(1, 1, 1)
    grad_w(1, 2, 0)
    grad_w(1, 2, 1)
    for copy in sm_b:
        copy.wait_recv()
    for g in range(2):
        for d in range(16):
            gf_out[g * 16 + d : g * 16 + d + 1, :] = sm[d // 4, d % 4, g : g + 1, :]
    skips = sm[0, 0, 4:8, :]
    for d in range(1, 16):
        skips = skips + sm[d // 4, d % 4, 4:8, :]
    gs_out[...] = skips
    bo_last(bo_b)

    for far in (False, True):
        for d in range(2):
            for i in range(2):
                ring[d, 1, far, i].wait_recv()
    own = zs[z]
    top = own[:256].astype(F32) + zr[0, 3].astype(F32) + zr[1, 6].astype(F32)
    low = own[256:].astype(F32) + zr[1, 3].astype(F32) + zr[0, 6].astype(F32)
    gx_out[:, :256] = top.T.astype(BF16)
    gx_out[:, 256:] = low.T.astype(BF16)
    for copy in sent:
        copy.wait_send()


def hand_on(*refs):
    came, out, sems = refs[:5], refs[5:10], refs[10]
    copies = [pltpu.make_async_copy(came[i], out[i], sems.at[i]) for i in range(5)]
    for copy in copies:
        copy.start()
    for copy in copies:
        copy.wait()


def per_device(block_in, w_in, filt, skip, grad_y):
    tokens = block_in.shape[0]
    scale = tokens ** (-0.5)
    vmem = pl.BlockSpec(memory_space=pltpu.VMEM)
    hbm = pl.BlockSpec(memory_space=pltpu.HBM)
    out_shape = (
        jax.ShapeDtypeStruct((128, 512), BF16),
        jax.ShapeDtypeStruct((128, 512), BF16),
        jax.ShapeDtypeStruct((3, 512, 512), F32),
        jax.ShapeDtypeStruct((32, 128), F32),
        jax.ShapeDtypeStruct((4, 128), F32),
    )
    scratch = [
        pltpu.VMEM((2048, 512), BF16),
        pltpu.VMEM((3, 512, 512), BF16),
        pltpu.VMEM((32, 128), F32),
        pltpu.VMEM((1, 512), F32),
        pltpu.VMEM((128, 512), BF16),
        pltpu.VMEM((3, 512, 512), BF16),
        pltpu.VMEM((512, 2048), BF16),
        pltpu.VMEM((2, 3, 4, 4, 16, 2048), BF16),
        pltpu.VMEM((2, 2, 2, 3, 3, 4, 16, QUARTER), BF16),
        pltpu.VMEM((2, 2, 2, 3, 3, 16, QUARTER), BF16),
        pltpu.VMEM((2, 3, 4, 4, 16, 2048), BF16),
        pltpu.VMEM((512, 2048), F32),
        pltpu.VMEM((4, 4, 2, 16, 128), BF16),
        pltpu.VMEM((2, 4, 4, 16, 128), BF16),
        pltpu.VMEM((4, 4, 2, 16, 128), BF16),
        pltpu.VMEM((4, 2, 4, 16, 128), BF16),
        pltpu.VMEM((4, 2, 4, 16, 128), BF16),
        pltpu.VMEM((4, 4, 2, 16, 128), BF16),
        pltpu.VMEM((4, 4, 8, 128), F32),
        pltpu.VMEM((8, 512, 128), BF16),
        pltpu.VMEM((8, 512, 128), BF16),
        pltpu.VMEM((8, 512, 128), BF16),
        pltpu.VMEM((2, 7, 256, 128), BF16),
        pltpu.SemaphoreType.DMA((N_SEMS,)),
        pltpu.SemaphoreType.DMA((N_SEMS,)),
        pltpu.SemaphoreType.DMA((9,)),
    ]
    results = pl.pallas_call(
        functools.partial(block_kernel, scale),
        out_shape=out_shape,
        in_specs=[hbm] * 5,
        out_specs=[vmem] * 5,
        scratch_shapes=scratch,
        compiler_params=pltpu.CompilerParams(
            collective_id=0, has_side_effects=True, vmem_limit_bytes=44 * 2**20
        ),
        cost_estimate=pl.CostEstimate(flops=10**10, bytes_accessed=10**7, transcendentals=0),
    )(*(pltpu.with_memory_space_constraint(a, pltpu.HBM) for a in (block_in, w_in, filt, skip.reshape(1, 512), grad_y)))
    block_out, grad_x, grad_w, grad_filt, grad_skip = pl.pallas_call(
        hand_on,
        out_shape=out_shape,
        in_specs=[vmem] * 5,
        out_specs=[pl.BlockSpec(memory_space=pl.ANY)] * 5,
        scratch_shapes=[pltpu.SemaphoreType.DMA((5,))],
        compiler_params=pltpu.CompilerParams(vmem_limit_bytes=8 * 2**20),
    )(*results)
    return block_out, grad_x, grad_w, grad_filt, grad_skip.reshape(512)


def solution(mesh):
    in_specs = (P(None, "seq"), P(None, "seq", "tp"), P("tp", None), P("tp"), P("seq", "tp"))
    out_specs = (P("seq", "tp"), P("tp", "seq"), P(None, "seq", "tp"), P("tp", None), P("tp"))
    return jax.shard_map(per_device, mesh=mesh, in_specs=in_specs, out_specs=out_specs, check_vma=False)
```
